32 devices in a mesh: tile: 8 (over z, y), layer: 4 (over x, core).
Axes of the slice: x: 2, y: 2, z: 4, core: 2. Of those that a mesh axis runs over, the one named last changes fastest.
Arguments:
- forcing: float32 [16, 16, 64, 512], P('layer', None, 'tile'), may hold values from -6 to 6
- vert_coupling: float32 [16, 64, 512], P(None, 'tile', 'layer'), may hold values from 0.25 to 4
- horiz_coupling: float32 [64, 512], P('tile'), may hold values from 0.25 to 2
- basal_velocity: float32 [64, 512], P('tile', 'layer'), may hold values from 0.5 to 10
- group_label: int32 [64, 512], P('tile', 'layer'), may hold values from 0 to 511
- ice_mask: int32 [64, 512], P('tile', 'layer'), may hold values 0 or 1
Outputs:
- adjoint: float32 [16, 16, 64, 512], P('layer', None, 'tile')
- sensitivity: float32 [16, 512], replicated
The draws below stay inside these ranges and needn't reach their ends.
All inputs are finite; a program needn't handle non-finite values. No bound on the sum of `ice_mask` on one device may be relied on, other than what follows from the above.
Results may differ from the reference program's by a relative error of at most 0.0001.
Values sent between devices are 32-bit elements; how exact they have to be, the bound alone decides.
No kernel may reach another device: no remote copies, remote signals or barrier semaphores. Data moves between devices by JAX's collectives and lax.ppermute only.
A program may use at most 64 MiB of HBM per device.

```python
import math
import jax
import jax.numpy as jnp
from jax import lax

F = 16
GROUPS = 512
NL = 16
SWEEPS = 2
RX = 512
NY = 64


def touch_ends(array, own_key, low, high):
    longest = array.shape.index(max(array.shape))
    spots = []
    for shift in (0, 1):
        where = [jax.random.randint(jax.random.fold_in(own_key, axis), (), 0, length) for axis, length in enumerate(array.shape)]
        where[longest] = (where[longest] + shift) % array.shape[longest]
        spots.append(tuple(where))
    return array.at[spots[0]].set(low).at[spots[1]].set(high)


def steps_of(rng, shape, cuts, low, high):
    loudness, own = 1.0, jax.random.fold_in(rng, 6)
    for axis_at, blocks in cuts:
        steps = jnp.exp(jax.random.uniform(jax.random.fold_in(own, axis_at), (blocks,), jnp.float32, low / len(cuts), high / len(cuts)))
        loudness = loudness * jnp.repeat(steps, shape[axis_at] // blocks).reshape([-1 if axis == axis_at else 1 for axis in range(len(shape))])
    return loudness


def normal_values(key, dims, width, most, pieces=(), kind=jnp.bfloat16):
    entries = jax.random.normal(key, dims, jnp.float32) * width
    if len(pieces) > 0:
        entries = steps_of(key, dims, pieces, -0.22, 0.18) * entries
    return jnp.clip(entries, min=-most, max=most).astype(kind)


def setup_inputs(seed: int = 0) -> dict:
    arg_keys = jax.random.split(jax.random.key(seed), 7)
    return {
        "forcing": normal_values(arg_keys[0], (NL, F, NY, RX), 1.0, 6.0, ((0, 4), (2, 8)), jnp.float32),
        "vert_coupling": jnp.clip(jnp.exp(math.log(4.0) - 2.7725887 * jax.random.uniform(arg_keys[1], (NL, NY, RX), jnp.float32) ** steps_of(arg_keys[1], (NL, NY, RX), ((1, 8), (2, 4)), -0.2, 0.2)), 0.25, 4.0),
        "horiz_coupling": jnp.clip(jnp.exp(math.log(2.0) - 2.0794415 * jax.random.uniform(arg_keys[2], (NY, RX), jnp.float32) ** steps_of(arg_keys[2], (NY, RX), ((0, 8),), -0.2, 0.2)), 0.25, 2.0),
        "basal_velocity": jnp.clip(jnp.exp(math.log(10.0) - 2.9957323 * jax.random.uniform(arg_keys[3], (NY, RX), jnp.float32) ** steps_of(arg_keys[3], (NY, RX), ((0, 8), (1, 4)), -0.2, 0.2)), 0.5, 10.0),
        "group_label": touch_ends(jax.random.randint(arg_keys[4], (NY, RX), 0, GROUPS), jax.random.fold_in(arg_keys[4], 1), 0, GROUPS - 1).astype(jnp.int32),
        "ice_mask": touch_ends((jax.random.randint(arg_keys[5], (NY, RX), 0, 4) < 3).astype(jnp.int32), jax.random.fold_in(arg_keys[5], 1), 0, 1),
    }


def column_solve(rhs, sub_diag, full_diag, super_diag):
    def forward(running, layer_in):
        c_prime, d_prime = running
        sub_k, diag_k, super_k, rhs_k = layer_in
        pivot = diag_k - sub_k * c_prime
        c_next = super_k / pivot
        d_next = (rhs_k - sub_k * d_prime) / pivot
        return (c_next, d_next), (c_next, d_next)

    start = (jnp.zeros_like(full_diag[0]), jnp.zeros_like(rhs[0]))
    _, (c_all, d_all) = lax.scan(forward, start, (sub_diag, full_diag, super_diag, rhs))

    def backward(solved_up, layer_in):
        c_here, d_here = layer_in
        solved = d_here - c_here * solved_up
        return solved, solved

    _, result = lax.scan(backward, jnp.zeros_like(rhs[0]), (c_all, d_all), reverse=True)
    return result


def vertical_apply(field, sub_diag, vert_diag, super_diag):
    zero_layer = jnp.zeros_like(field[:1])
    below = jnp.concatenate([zero_layer, field[:-1]], axis=0)
    above = jnp.concatenate([field[1:], zero_layer], axis=0)
    return vert_diag * field + sub_diag * below + super_diag * above


def reference(forcing, vert_coupling, horiz_coupling, basal_velocity, group_label, ice_mask):
    zero_layer = jnp.zeros_like(vert_coupling[:1])
    coupling_next = jnp.concatenate([vert_coupling[1:], zero_layer], axis=0)
    sub_diag = jnp.concatenate([zero_layer, -vert_coupling[1:]], axis=0)
    super_diag = -coupling_next
    vert_diag = vert_coupling + coupling_next
    full_diag = vert_diag + 4.0 * horiz_coupling

    def horizontal(field):
        padded = jnp.pad(field, ((0, 0), (1, 1), (1, 1)))
        return horiz_coupling * (4.0 * field - padded[:, :-2, 1:-1] - padded[:, 2:, 1:-1]
                                 - padded[:, 1:-1, :-2] - padded[:, 1:-1, 2:])

    def solve_single(forcing_one):
        adjoint_one = column_solve(forcing_one, sub_diag, full_diag, super_diag)
        for sweep in range(SWEEPS - 1):
            residual = forcing_one - (horizontal(adjoint_one) + vertical_apply(adjoint_one, sub_diag, vert_diag, super_diag))
            adjoint_one = adjoint_one + column_solve(residual, sub_diag, full_diag, super_diag)
        return adjoint_one

    adjoint_all = lax.map(solve_single, jnp.moveaxis(forcing, 1, 0))
    adjoint = jnp.moveaxis(adjoint_all, 0, 1)
    weight = vert_coupling[0] * basal_velocity * ice_mask.astype(jnp.float32)
    weighted = (adjoint_all[:, 0] * weight).reshape(F, NY * RX)
    totals = jax.ops.segment_sum(weighted.T, group_label.reshape(-1).astype(jnp.int32), num_segments=GROUPS)
    sensitivity = -totals.T * ((NY * RX / GROUPS) ** -0.5)
    return adjoint, sensitivity
```

```python
import functools

import jax
import jax.numpy as jnp
from jax import lax
from jax.experimental import pallas as pl
from jax.experimental.pallas import tpu as pltpu
from jax.sharding import PartitionSpec as P

GROUPS = 512
LANES = 128
VMEM_BYTES = 48 * 1024 * 1024
UP, DOWN, LEFT, RIGHT = range(4)


def position():
    layer = lax.axis_index("layer")
    return layer // 2, layer % 2


def edge_flags():
    tile = lax.axis_index("tile")
    last = lax.axis_size("tile") - 1
    return (
        jnp.where(tile > 0, 1.0, 0.0).astype(jnp.float32),
        jnp.where(tile < last, 1.0, 0.0).astype(jnp.float32),
    )


def moved(plane, direction, halo=None):
    rows, width = plane.shape
    axis = 0 if direction in (UP, DOWN) else 1
    size = plane.shape[axis]
    first = direction in (UP, LEFT)
    rolled = pltpu.roll(plane, 1 if first else size - 1, axis)
    at_edge = lax.broadcasted_iota(jnp.int32, plane.shape, axis) == (0 if first else size - 1)
    filler = jnp.zeros_like(plane) if halo is None else jnp.broadcast_to(halo, plane.shape)
    return jnp.where(at_edge, filler, rolled)


def chip_factors(planes, side, layers):
    half = layers // 2
    horiz = planes(layers + 2)

    def coupling(j):
        if j == 0:
            return planes(0) * jnp.where(side == 0, 1.0, 0.0)
        return planes(jnp.where(side == 0, j, layers - j))

    multiplier, inverse = [None], []
    below = coupling(0)
    for j in range(half):
        above = coupling(j + 1)
        pivot = below + above + 4.0 * horiz
        if j > 0:
            pivot = pivot - below * multiplier[j]
        inverse.append(1.0 / pivot)
        multiplier.append(above * inverse[j])
        below = above
    return multiplier, inverse, below


def unit_response(multiplier, inverse):
    half = len(inverse)
    response = [None] * half
    response[half - 1] = inverse[half - 1]
    for j in range(half - 2, -1, -1):
        response[j] = multiplier[j + 1] * response[j + 1]
    return response


def chip_solve(values, multiplier, inverse):
    half = len(values)
    swept = [values[0]]
    for j in range(1, half):
        swept.append(values[j] + multiplier[j] * swept[j - 1])
    solved = [None] * half
    solved[half - 1] = swept[half - 1] * inverse[half - 1]
    for j in range(half - 2, -1, -1):
        solved[j] = swept[j] * inverse[j] + multiplier[j + 1] * solved[j + 1]
    return solved


def assemble_kernel(own, peer, cross, diag, horiz, planes, row_first, row_last):
    layer = lax.axis_index("layer")
    count = own.shape[0]
    for k, block in enumerate((own, peer, cross, diag)):
        start = pl.multiple_of(jnp.bitwise_xor(layer, k) * LANES, LANES)
        planes[0:count, :, pl.ds(start, LANES)] = block[...]
    planes[count] = horiz[...]
    rows = planes.shape[1]
    for k in range(count + 1):
        row_first[k : k + 1, :] = planes[k, 0:1, :]
        row_last[k : k + 1, :] = planes[k, rows - 1 : rows, :]
    for k in range(count + 1, row_first.shape[0]):
        row_first[k : k + 1, :] = planes[0, 0:1, :]
        row_last[k : k + 1, :] = planes[0, 0:1, :]


def load_forcing(own, received, gathered, sems):
    _, core = position()
    held, functionals = received.shape[0], received.shape[1]
    copies = (
        pltpu.make_async_copy(
            own.at[:, pl.ds(core * functionals, functionals)],
            gathered.at[pl.ds(core * held, held)],
            sems.at[0],
        ),
        pltpu.make_async_copy(received, gathered.at[pl.ds((1 - core) * held, held)], sems.at[1]),
    )
    for copy in copies:
        copy.start()
    return copies


def local_kernel(own, received, planes, local, boundary, row_first, row_last, gathered, factors, sems):
    side, _ = position()
    copies = load_forcing(own, received, gathered, sems)
    layers = planes.shape[0] - 3
    half, functionals, rows, _ = local.shape
    multiplier, inverse, _ = chip_factors(lambda k: planes[k], side, layers)
    for j in range(half):
        factors[0, j] = multiplier[j + 1]
        factors[1, j] = inverse[j]
    for copy in copies:
        copy.wait()

    def step(f, carry):
        values = [gathered[side * (half - 1) + (1 - 2 * side) * j, f] for j in range(half)]
        solved = chip_solve(
            values,
            [None] + [factors[0, j] for j in range(half)],
            [factors[1, j] for j in range(half)],
        )
        for j in range(half):
            local[j, f] = solved[j]
            row_first[pl.ds(j * functionals + f, 1), :] = solved[j][0:1]
            row_last[pl.ds(j * functionals + f, 1), :] = solved[j][rows - 1 : rows]
        boundary[f] = solved[half - 1]
        return carry

    lax.fori_loop(0, functionals, step, 0)


def column_kernel(own, received, planes, above, below, sums, gathered, weights, halo, terms, outer, sems, *, scale):
    side, core = position()
    copies = load_forcing(own, received, gathered, sems)
    layers = planes.shape[0] - 3
    half, functionals, rows, width = gathered.shape
    has_above, has_below = edge_flags()
    top_row = lax.broadcasted_iota(jnp.int32, halo.shape[1:], 0) == 0
    for k in range(layers + 3):
        halo[k] = jnp.where(
            top_row,
            jnp.broadcast_to(above[k : k + 1, :], halo.shape[1:]),
            jnp.broadcast_to(below[k : k + 1, :], halo.shape[1:]),
        )
    halo_live = jnp.where(top_row, has_above, has_below)

    def factor(get):
        multiplier, inverse = [None], []
        horiz = get(layers + 2)
        low = get(0)
        for k in range(layers):
            high = get(k + 1) if k + 1 < layers else jnp.zeros_like(low)
            pivot = low + high + 4.0 * horiz
            if k > 0:
                pivot = pivot - low * multiplier[k]
            inverse.append(1.0 / pivot)
            multiplier.append(high * inverse[k])
            low = high
        return multiplier, inverse

    def bed_row(multiplier, inverse):
        swept = [jnp.ones_like(inverse[0])]
        for k in range(1, layers):
            swept.append(multiplier[k] * swept[k - 1])
        solved = [None] * layers
        solved[layers - 1] = swept[layers - 1] * inverse[layers - 1]
        for k in range(layers - 2, -1, -1):
            solved[k] = swept[k] * inverse[k] + multiplier[k + 1] * solved[k + 1]
        return solved

    halo_multiplier, halo_inverse = factor(lambda k: halo[k])
    halo_scale = halo[layers] * halo[layers + 2] * halo_live
    for k, value in enumerate(bed_row(halo_multiplier, halo_inverse)):
        halo[k] = value * halo_scale
    multiplier, inverse = factor(lambda k: planes[k])
    weight = planes[layers]
    spread = weight * planes[layers + 2]
    for k, value in enumerate(bed_row(multiplier, inverse)):
        weights[4, k] = value
    for direction in (UP, DOWN, LEFT, RIGHT):
        source = []
        for k in range(layers):
            edge = None
            if direction == UP:
                edge = halo[k, 0:1, :]
            if direction == DOWN:
                edge = halo[k, 1:2, :]
            source.append(moved(weights[4, k] * spread, direction, edge))
        for k, value in enumerate(chip_solve(source, multiplier, inverse)):
            weights[direction, k] = value
    for k in range(layers):
        weights[4, k] = weights[4, k] * weight
    for copy in copies:
        copy.wait()

    def step(f, carry):
        values = [gathered[m, f] for m in range(half)]

        def total(kind):
            out = values[0] * weights[kind, side * half]
            for m in range(1, half):
                out = out + values[m] * weights[kind, side * half + m]
            return out

        to_up, to_down = total(UP), total(DOWN)
        here = total(4) + moved(to_up, DOWN) + moved(to_down, UP)
        here = here + moved(total(LEFT), RIGHT) + moved(total(RIGHT), LEFT)
        terms[f] = here
        outer[0, pl.ds(f, 1), :] = to_up[0:1]
        outer[1, pl.ds(f, 1), :] = to_down[rows - 1 : rows]
        return carry

    lax.fori_loop(0, functionals, step, 0)

    groups_low = lax.broadcasted_iota(jnp.int32, (LANES, width), 0)
    blocks = GROUPS // LANES

    def grouped(values, labels):
        label = labels.astype(jnp.int32)
        parts = []
        for b in range(blocks):
            inside = jnp.broadcast_to((label // LANES) == b, values.shape)
            parts.append(jnp.where(inside, values, 0.0))
        left = jnp.concatenate(parts, axis=0)
        high = left.astype(jnp.bfloat16)
        rest = left - high.astype(jnp.float32)
        middle = rest.astype(jnp.bfloat16)
        low = (rest - middle.astype(jnp.float32)).astype(jnp.bfloat16)
        left = jnp.concatenate([high, middle, low], axis=0)
        match = jnp.where(jnp.broadcast_to(label % LANES, groups_low.shape) == groups_low, 1.0, 0.0)
        return lax.dot_general(
            left,
            match.astype(jnp.bfloat16),
            (((1,), (1,)), ((), ())),
            preferred_element_type=jnp.float32,
        )

    total = grouped(outer[0], above[layers + 1 : layers + 2, :])
    total = total + grouped(outer[1], below[layers + 1 : layers + 2, :])
    for y in range(rows):
        total = total + grouped(terms[:, y, :], planes[layers + 1, y : y + 1, :])
    size = blocks * functionals
    total = (total[0:size] + total[size : 2 * size] + total[2 * size :]) * scale
    sums[...] = jnp.zeros_like(sums)
    start = pl.multiple_of(core * functionals, functionals)
    for b in range(blocks):
        sums[pl.ds(start, functionals), b * LANES : (b + 1) * LANES] = total[
            b * functionals : (b + 1) * functionals
        ]


def middle_kernel(local, planes, halo_up, halo_down, base, message, factors):
    side, _ = position()
    layers = planes.shape[0] - 3
    half, functionals, rows, _ = local.shape
    has_above, has_below = edge_flags()
    multiplier, inverse, _ = chip_factors(lambda k: planes[k], side, layers)
    for j in range(half):
        factors[0, j] = multiplier[j + 1]
        factors[1, j] = inverse[j]
    inner = (half - 1) * functionals
    message[functionals * rows : functionals * (rows + 1), :] = halo_up[inner : inner + functionals, :]
    message[functionals * (rows + 1) :, :] = halo_down[inner : inner + functionals, :]

    def step(f, carry):
        horiz = planes[layers + 2]
        residual = []
        for j in range(half):
            here = local[j, f]
            around = moved(here, UP, halo_up[pl.ds(j * functionals + f, 1), :] * has_above)
            around = around + moved(here, DOWN, halo_down[pl.ds(j * functionals + f, 1), :] * has_below)
            around = around + moved(here, LEFT) + moved(here, RIGHT)
            residual.append(horiz * around)
        solved = chip_solve(
            residual,
            [None] + [factors[0, j] for j in range(half)],
            [factors[1, j] for j in range(half)],
        )
        for j in range(half):
            solved[j] = local[j, f] + solved[j]
            base[j, f] = solved[j]
        message[pl.ds(pl.multiple_of(f * rows, rows), rows), :] = solved[half - 1]
        return carry

    lax.fori_loop(0, functionals, step, 0)


def coefficient_kernel(planes, above, below, spread, spread_other, response, ends, halo, halo_response):
    side, _ = position()
    layers = planes.shape[0] - 3
    half = layers // 2
    has_above, has_below = edge_flags()
    top_row = lax.broadcasted_iota(jnp.int32, halo.shape[1:], 0) == 0
    for k in range(layers + 3):
        halo[k] = jnp.where(
            top_row,
            jnp.broadcast_to(above[k : k + 1, :], halo.shape[1:]),
            jnp.broadcast_to(below[k : k + 1, :], halo.shape[1:]),
        )
    halo_live = jnp.where(top_row, has_above, has_below)

    def both(get):
        multiplier, inverse, kappa = chip_factors(get, side, layers)
        unit = unit_response(multiplier, inverse)
        multiplier_other, inverse_other, _ = chip_factors(get, 1 - side, layers)
        unit_other = unit_response(multiplier_other, inverse_other)
        mine, other = kappa * unit[half - 1], kappa * unit_other[half - 1]
        return multiplier, inverse, kappa, unit, unit_other, (mine, other, 1.0 / (1.0 - mine * other))

    _, _, kappa, unit, unit_other, corner = both(lambda k: halo[k])
    rows_halo = halo.shape[1]
    for i in range(3):
        ends[i + 3, 0:rows_halo] = corner[i] * halo_live if i == 2 else corner[i]
    for j in range(half):
        halo_response[0, j] = kappa * unit[j] * halo_live
        halo_response[1, j] = kappa * unit_other[j] * halo_live
    multiplier, inverse, kappa, unit, unit_other, corner = both(lambda k: planes[k])
    for i in range(3):
        ends[i] = corner[i]
    horiz = planes[layers + 2]
    mine = [kappa * unit[j] for j in range(half)]
    other = [kappa * unit_other[j] for j in range(half)]
    for j in range(half):
        response[j] = mine[j]
    for direction in (UP, DOWN, LEFT, RIGHT):
        source, total = [], jnp.zeros_like(horiz)
        for j in range(half):
            edges = (None, None)
            if direction in (UP, DOWN):
                edges = tuple(halo_response[i, j, direction : direction + 1, :] for i in range(2))
            source.append(horiz * moved(mine[j], direction, edges[0]))
            total = total + unit_other[j] * moved(other[j], direction, edges[1])
        spread_other[direction] = horiz * total
        for j, value in enumerate(chip_solve(source, multiplier, inverse)):
            spread[direction, j] = value


def final_kernel(
    base, boundary, boundary_other, message, halo_up, halo_down, spread, spread_other, response, ends,
    kept, sent, halo_mine, halo_other,
):
    side, core = position()
    half, functionals, rows, _ = base.shape
    held = half // 2
    inner = (half - 1) * functionals
    for i, rows_in in enumerate((halo_up, halo_down)):
        near = rows_in[inner : inner + functionals, :]
        start = functionals * (rows + i)
        far = message[start : start + functionals, :]
        mine, other, inverse = (ends[k, i : i + 1, :] for k in (3, 4, 5))
        live = jnp.where(inverse == 0.0, 0.0, 1.0)
        value = (far + other * near) * inverse
        halo_other[i] = value
        halo_mine[i] = (near + mine * value) * live

    def step(f, carry):
        near = boundary[f]
        mine, other, inverse = ends[0], ends[1], ends[2]
        value = (boundary_other[f] + other * near) * inverse
        value_mine = near + mine * value

        def around(plane, edges):
            return [
                moved(plane, UP, edges[0, pl.ds(f, 1), :]),
                moved(plane, DOWN, edges[1, pl.ds(f, 1), :]),
                moved(plane, LEFT),
                moved(plane, RIGHT),
            ]

        value_around = around(value, halo_other)
        mine_around = around(value_mine, halo_mine)
        last = base[half - 1, f]
        last_other = message[pl.ds(pl.multiple_of(f * rows, rows), rows), :]
        for d in range(4):
            last = last + spread[d, half - 1] * value_around[d]
            last_other = last_other + spread_other[d] * mine_around[d]
        second = (last_other + other * last) * inverse
        for group in range(2):
            solved = []
            for i in range(held):
                m = group * held + i
                j = jnp.where(side == 0, m, half - 1 - m)
                out = base[j, f] + response[j] * second
                for d in range(4):
                    out = out + spread[d, j] * value_around[d]
                solved.append(out)

            @pl.when(core == group)
            def _():
                for i in range(held):
                    kept[i, core * functionals + f] = solved[i]

            @pl.when(core != group)
            def _():
                for i in range(held):
                    sent[i, f] = solved[i]

        return carry

    lax.fori_loop(0, functionals, step, 0)


def call(kernel, out_shapes, scratch=(), any_inputs=0, **cost):
    def run(*operands):
        in_specs = [
            pl.BlockSpec(memory_space=pl.ANY if i < any_inputs else pltpu.VMEM)
            for i in range(len(operands))
        ]
        return pl.pallas_call(
            kernel,
            out_shape=[jax.ShapeDtypeStruct(s, jnp.float32) for s in out_shapes],
            in_specs=in_specs,
            out_specs=[pl.BlockSpec(memory_space=pltpu.VMEM) for _ in out_shapes],
            scratch_shapes=list(scratch),
            compiler_params=pltpu.CompilerParams(vmem_limit_bytes=VMEM_BYTES),
            cost_estimate=pl.CostEstimate(
                flops=cost.get("flops", 1000000), bytes_accessed=2000000, transcendentals=0
            ),
        )(*operands)

    return run


def shards(forcing, vert_coupling, horiz_coupling, basal_velocity, group_label, ice_mask):
    layers, rows, width_block = vert_coupling.shape
    held, functionals_all, _, width = forcing.shape
    half, functionals = layers // 2, functionals_all // 2
    tiles = lax.axis_size("tile")
    core = lax.axis_index("layer") % 2
    f32 = jnp.float32

    def across(array, bits):
        return lax.ppermute(array, "layer", [(i, i ^ bits) for i in range(4)])

    def to_next(array):
        return lax.ppermute(array, "tile", [(i, (i + 1) % tiles) for i in range(tiles)])

    def to_previous(array):
        return lax.ppermute(array, "tile", [((i + 1) % tiles, i) for i in range(tiles)])

    weight = vert_coupling[0] * basal_velocity * ice_mask.astype(f32)
    block = jnp.concatenate([vert_coupling, weight[None], group_label.astype(f32)[None]], axis=0)
    block_cross = across(block, 2)
    block_peer = across(block, 1)
    forcing_sent = lax.dynamic_slice_in_dim(forcing, (1 - core) * functionals, functionals, 1)
    forcing_received = across(forcing_sent, 1)
    block_diag = across(block_cross, 1)

    count = layers + 3
    edge_rows = -(-count // 8) * 8
    planes, plane_first, plane_last = call(
        assemble_kernel, [(count, rows, width), (edge_rows, width), (edge_rows, width)]
    )(block, block_peer, block_cross, block_diag, horiz_coupling)
    above = to_next(plane_last)
    below = to_previous(plane_first)

    gathered = pltpu.VMEM((half, functionals, rows, width), f32)
    factors = pltpu.VMEM((2, half, rows, width), f32)
    stack = half * functionals
    local, boundary, local_first, local_last = call(
        local_kernel,
        [(half, functionals, rows, width), (functionals, rows, width), (stack, width), (stack, width)],
        [gathered, factors, pltpu.SemaphoreType.DMA((2,))],
        any_inputs=2,
    )(forcing, forcing_received, planes)
    boundary_other = across(boundary, 2)
    halo_up = to_next(local_last)
    halo_down = to_previous(local_first)

    columns_all = tiles * rows * width
    halo_planes = pltpu.VMEM((count, 8, width), f32)
    (sums,) = call(
        functools.partial(column_kernel, scale=-((columns_all / GROUPS) ** -0.5)),
        [(functionals_all, GROUPS)],
        [
            gathered,
            pltpu.VMEM((5, layers, rows, width), f32),
            halo_planes,
            pltpu.VMEM((functionals, rows, width), f32),
            pltpu.VMEM((2, functionals, width), f32),
            pltpu.SemaphoreType.DMA((2,)),
        ],
        any_inputs=2,
    )(forcing, forcing_received, planes, above, below)

    sums = sums + across(sums, 1)
    sums = sums + across(sums, 3)
    step = 1
    while step < tiles:
        pairs = [(4 * t + i, 4 * (t ^ step) + (i ^ 1)) for t in range(tiles) for i in range(4)]
        sums = sums + lax.ppermute(sums, ("tile", "layer"), pairs)
        step *= 2

    spread, spread_other, response, ends = call(
        coefficient_kernel,
        [(4, half, rows, width), (4, rows, width), (half, rows, width), (6, rows, width)],
        [halo_planes, pltpu.VMEM((2, half, 8, width), f32)],
    )(planes, above, below)

    base, message = call(
        middle_kernel,
        [(half, functionals, rows, width), (functionals * (rows + 2), width)],
        [factors],
    )(local, planes, halo_up, halo_down)
    message_other = across(message, 2)

    kept, sent = call(
        final_kernel,
        [(held, functionals_all, rows, width), (held, functionals, rows, width)],
        [pltpu.VMEM((2, functionals, width), f32), pltpu.VMEM((2, functionals, width), f32)],
    )(base, boundary, boundary_other, message_other, halo_up, halo_down, spread, spread_other, response, ends)
    received = across(sent, 1)
    adjoint = lax.dynamic_update_slice_in_dim(kept, received, (1 - core) * functionals, 1)
    return (adjoint, sums)


def solution(mesh):
    in_specs = (
        P("layer", None, "tile", None),
        P(None, "tile", "layer"),
        P("tile", None),
        P("tile", "layer"),
        P("tile", "layer"),
        P("tile", "layer"),
    )
    out_specs = (P("layer", None, "tile", None), P())
    return jax.shard_map(shards, mesh=mesh, in_specs=in_specs, out_specs=out_specs, check_vma=False)
```

```python
import functools

import jax
import jax.numpy as jnp
from jax import lax
from jax.experimental import pallas as pl
from jax.experimental.pallas import tpu as pltpu
from jax.sharding import PartitionSpec as P

GROUPS = 512
LANES = 128
VMEM_BYTES = 32 * 1024 * 1024
UP, DOWN, LEFT, RIGHT = range(4)


def position():
    layer = lax.axis_index("layer")
    return layer // 2, layer % 2


def owned_half():
    side, core = position()
    tile = lax.axis_index("tile")
    total = side + core
    for bit in range((lax.axis_size("tile") - 1).bit_length()):
        total = total + lax.shift_right_logical(tile, bit) % 2
    return total % 2


def edge_flags():
    tile = lax.axis_index("tile")
    last = lax.axis_size("tile") - 1
    return (
        jnp.where(tile > 0, 1.0, 0.0).astype(jnp.float32),
        jnp.where(tile < last, 1.0, 0.0).astype(jnp.float32),
    )


def paired_rows(first, last):
    even = lax.axis_index("tile") % 2 == 0
    return jnp.where(even, last, first), jnp.where(even, first, last)


def halo_rows(near, far):
    even = lax.axis_index("tile") % 2 == 0
    return jnp.where(even, far, near), jnp.where(even, near, far)


def moved(plane, direction, halo=None):
    rows, width = plane.shape
    axis = 0 if direction in (UP, DOWN) else 1
    size = plane.shape[axis]
    first = direction in (UP, LEFT)
    rolled = pltpu.roll(plane, 1 if first else size - 1, axis)
    at_edge = lax.broadcasted_iota(jnp.int32, plane.shape, axis) == (0 if first else size - 1)
    filler = jnp.zeros_like(plane) if halo is None else jnp.broadcast_to(halo, plane.shape)
    return jnp.where(at_edge, filler, rolled)


def chip_factors(planes, side, layers):
    half = layers // 2
    horiz = planes(layers + 2)

    def coupling(j):
        if j == 0:
            return planes(0) * jnp.where(side == 0, 1.0, 0.0)
        return planes(jnp.where(side == 0, j, layers - j))

    multiplier, inverse = [None], []
    below = coupling(0)
    for j in range(half):
        above = coupling(j + 1)
        pivot = below + above + 4.0 * horiz
        if j > 0:
            pivot = pivot - below * multiplier[j]
        inverse.append(1.0 / pivot)
        multiplier.append(above * inverse[j])
        below = above
    return multiplier, inverse, below


def unit_response(multiplier, inverse):
    half = len(inverse)
    response = [None] * half
    response[half - 1] = inverse[half - 1]
    for j in range(half - 2, -1, -1):
        response[j] = multiplier[j + 1] * response[j + 1]
    return response


def chip_solve(values, multiplier, inverse):
    half = len(values)
    swept = [values[0]]
    for j in range(1, half):
        swept.append(values[j] + multiplier[j] * swept[j - 1])
    solved = [None] * half
    solved[half - 1] = swept[half - 1] * inverse[half - 1]
    for j in range(half - 2, -1, -1):
        solved[j] = swept[j] * inverse[j] + multiplier[j + 1] * solved[j + 1]
    return solved


def pack_kernel(
    coupling, velocity, label, mask, forcing, block, sent, kept, velocity_in, label_in, mask_in, sems
):
    mine = owned_half()
    layers = coupling.shape[0]
    functionals = sent.shape[1]
    pairs = [
        (coupling, block.at[pl.ds(0, layers)]),
        (velocity, velocity_in),
        (label, label_in),
        (mask, mask_in),
    ]
    for target, which in ((sent, 1 - mine), (kept, mine)):
        pairs.append((forcing.at[:, pl.ds(which * functionals, functionals)], target))
    copies = [pltpu.make_async_copy(a, b, sems.at[i]) for i, (a, b) in enumerate(pairs)]
    for copy in copies:
        copy.start()
    for copy in copies[:4]:
        copy.wait()
    block[layers] = block[0] * velocity_in[...] * mask_in[...].astype(jnp.float32)
    block[layers + 1] = label_in[...].astype(jnp.float32)
    for copy in copies[4:]:
        copy.wait()


def place_kernel(kept, received, mine_sums, other_sums, out, sums, sems):
    mine = owned_half()
    functionals = kept.shape[1]
    copies = []
    for i, (source, group, which) in enumerate(((received, other_sums, 1 - mine), (kept, mine_sums, mine))):
        at = pl.ds(pl.multiple_of(which * functionals, functionals), functionals)
        copies.append(pltpu.make_async_copy(source, out.at[:, at], sems.at[2 * i]))
        copies.append(pltpu.make_async_copy(group, sums.at[at], sems.at[2 * i + 1]))
    for copy in copies:
        copy.start()
    for copy in copies:
        copy.wait()


def assemble_kernel(own, peer, cross, diag, horiz, planes, row_near, row_far):
    layer = lax.axis_index("layer")
    count, rows = own.shape[0], own.shape[1]
    for k, block in ((0, own), (1, peer), (3, cross), (2, diag)):
        start = pl.multiple_of(jnp.bitwise_xor(layer, k) * LANES, LANES)
        planes[0:count, :, pl.ds(start, LANES)] = block[...]
    planes[count] = horiz[...]
    for k in range(row_near.shape[0]):
        at = min(k, count)
        near, far = paired_rows(planes[at, 0:1, :], planes[at, rows - 1 : rows, :])
        row_near[k : k + 1, :] = near
        row_far[k : k + 1, :] = far


def load_forcing(own, received, gathered, sems):
    _, core = position()
    held = received.shape[0]
    copies = (
        pltpu.make_async_copy(own, gathered.at[pl.ds(core * held, held)], sems.at[0]),
        pltpu.make_async_copy(received, gathered.at[pl.ds((1 - core) * held, held)], sems.at[1]),
    )
    for copy in copies:
        copy.start()
    return copies


def local_kernel(own, received, planes, local, boundary, row_near, row_far, gathered, factors, sems):
    side, _ = position()
    copies = load_forcing(own, received, gathered, sems)
    layers = planes.shape[0] - 3
    half, functionals, rows, _ = local.shape
    multiplier, inverse, _ = chip_factors(lambda k: planes[k], side, layers)
    for j in range(half):
        factors[0, j] = multiplier[j + 1]
        factors[1, j] = inverse[j]
    for copy in copies:
        copy.wait()

    def step(f, carry):
        values = [gathered[side * (half - 1) + (1 - 2 * side) * j, f] for j in range(half)]
        solved = chip_solve(
            values,
            [None] + [factors[0, j] for j in range(half)],
            [factors[1, j] for j in range(half)],
        )
        for j in range(half):
            local[j, f] = solved[j]
            near, far = paired_rows(solved[j][0:1], solved[j][rows - 1 : rows])
            row_near[pl.ds(j * functionals + f, 1), :] = near
            row_far[pl.ds(j * functionals + f, 1), :] = far
        boundary[f] = solved[half - 1]
        return carry

    lax.fori_loop(0, functionals, step, 0)


def full_factors(get, layers):
    multiplier, inverse = [None], []
    horiz = get(layers + 2)
    low = get(0)
    for k in range(layers):
        high = get(k + 1) if k + 1 < layers else jnp.zeros_like(low)
        pivot = low + high + 4.0 * horiz
        if k > 0:
            pivot = pivot - low * multiplier[k]
        inverse.append(1.0 / pivot)
        multiplier.append(high * inverse[k])
        low = high
    return multiplier, inverse


def bed_row(multiplier, inverse):
    layers = len(inverse)
    swept = [jnp.ones_like(inverse[0])]
    for k in range(1, layers):
        swept.append(multiplier[k] * swept[k - 1])
    solved = [None] * layers
    solved[layers - 1] = swept[layers - 1] * inverse[layers - 1]
    for k in range(layers - 2, -1, -1):
        solved[k] = swept[k] * inverse[k] + multiplier[k + 1] * solved[k + 1]
    return solved


def grouped(values, labels):
    label = labels.astype(jnp.int32)
    parts = []
    for b in range(GROUPS // LANES):
        inside = jnp.broadcast_to((label // LANES) == b, values.shape)
        parts.append(jnp.where(inside, values, 0.0))
    left = jnp.concatenate(parts, axis=0)
    high = left.astype(jnp.bfloat16)
    rest = left - high.astype(jnp.float32)
    middle = rest.astype(jnp.bfloat16)
    low = (rest - middle.astype(jnp.float32)).astype(jnp.bfloat16)
    left = jnp.concatenate([high, middle, low], axis=0)
    place = lax.broadcasted_iota(jnp.int32, (LANES, values.shape[1]), 0)
    match = jnp.where(jnp.broadcast_to(label % LANES, place.shape) == place, 1.0, 0.0)
    return lax.dot_general(
        left,
        match.astype(jnp.bfloat16),
        (((1,), (1,)), ((), ())),
        preferred_element_type=jnp.float32,
    )


def add_groups(sums, total, scale, functionals):
    blocks = GROUPS // LANES
    size = blocks * functionals
    total = (total[0:size] + total[size : 2 * size] + total[2 * size :]) * scale
    for b in range(blocks):
        lanes = slice(b * LANES, (b + 1) * LANES)
        sums[:, lanes] = sums[:, lanes] + total[b * functionals : (b + 1) * functionals]


def column_kernel(own, received, planes, sums, gathered, weights, terms, sems, *, scale):
    side, core = position()
    copies = load_forcing(own, received, gathered, sems)
    layers = planes.shape[0] - 3
    half, functionals, rows, _ = gathered.shape
    multiplier, inverse = full_factors(lambda k: planes[k], layers)
    weight = planes[layers]
    spread = weight * planes[layers + 2]
    for k, value in enumerate(bed_row(multiplier, inverse)):
        weights[4, k] = value
    for direction in (UP, DOWN, LEFT, RIGHT):
        source = [moved(weights[4, k] * spread, direction) for k in range(layers)]
        for k, value in enumerate(chip_solve(source, multiplier, inverse)):
            weights[direction, k] = value
    for k in range(layers):
        weights[4, k] = weights[4, k] * weight
    for copy in copies:
        copy.wait()

    def step(f, carry):
        values = [gathered[m, f] for m in range(half)]

        def total(kind):
            out = values[0] * weights[kind, side * half]
            for m in range(1, half):
                out = out + values[m] * weights[kind, side * half + m]
            return out

        here = total(4) + moved(total(UP), DOWN) + moved(total(DOWN), UP)
        terms[f] = here + moved(total(LEFT), RIGHT) + moved(total(RIGHT), LEFT)
        return carry

    lax.fori_loop(0, functionals, step, 0)
    total = grouped(terms[:, 0, :], planes[layers + 1, 0:1, :])
    for y in range(1, rows):
        total = total + grouped(terms[:, y, :], planes[layers + 1, y : y + 1, :])
    sums[...] = jnp.zeros_like(sums)
    add_groups(sums, total, scale, functionals)


def border_kernel(own, received, planes, near, far, inside, sums, halo, *, scale):
    side, core = position()
    layers = planes.shape[0] - 3
    held, functionals, rows, width = received.shape
    top_row = lax.broadcasted_iota(jnp.int32, halo.shape[1:], 0) == 0
    has_above, has_below = edge_flags()

    def pair(above, below):
        return jnp.where(
            top_row, jnp.broadcast_to(above, halo.shape[1:]), jnp.broadcast_to(below, halo.shape[1:])
        )

    for k in range(layers + 3):
        halo[k] = pair(*halo_rows(near[k : k + 1, :], far[k : k + 1, :]))
    outer = bed_row(*full_factors(lambda k: halo[k], layers))
    live = halo[layers] * halo[layers + 2] * jnp.where(top_row, has_above, has_below)
    edge = full_factors(lambda k: pair(planes[k, 0:1, :], planes[k, rows - 1 : rows, :]), layers)
    solved = chip_solve([value * live for value in outer], *edge)
    sums[...] = inside[...]
    total = None
    for which, row in enumerate((0, rows - 1)):
        out = None
        for m in range(2 * held):
            weight = jnp.where(side == 0, solved[m][which : which + 1], solved[2 * held + m][which : which + 1])
            mine, other = own[m % held, :, row, :], received[m % held, :, row, :]
            value = jnp.where(core == m // held, mine, other) * weight
            out = value if out is None else out + value
        part = grouped(out, halo[layers + 1, which : which + 1, :])
        total = part if total is None else total + part
    add_groups(sums, total, scale, functionals)


def fold_kernel(mine, *refs):
    parts, message, out = refs[:-2], refs[-2], refs[-1]
    total = mine[...]
    if parts:
        total = total + parts[0][...]
    if len(parts) == 3:
        total = total + (parts[1][...] + parts[2][...])
    size = mine.shape[0]
    out[out.shape[0] - size :, :] = total


def middle_kernel(local, planes, near, far, base, message, factors):
    side, _ = position()
    layers = planes.shape[0] - 3
    half, functionals, rows, _ = local.shape
    has_above, has_below = edge_flags()
    multiplier, inverse, _ = chip_factors(lambda k: planes[k], side, layers)
    for j in range(half):
        factors[0, j] = multiplier[j + 1]
        factors[1, j] = inverse[j]
    inner = (half - 1) * functionals
    above, below = halo_rows(near[inner : inner + functionals, :], far[inner : inner + functionals, :])
    message[functionals * rows : functionals * (rows + 1), :] = above
    message[functionals * (rows + 1) : functionals * (rows + 2), :] = below

    def step(f, carry):
        horiz = planes[layers + 2]
        residual = []
        for j in range(half):
            here = local[j, f]
            at = pl.ds(j * functionals + f, 1)
            above, below = halo_rows(near[at, :], far[at, :])
            around = moved(here, UP, above * has_above) + moved(here, DOWN, below * has_below)
            around = around + moved(here, LEFT) + moved(here, RIGHT)
            residual.append(horiz * around)
        solved = chip_solve(
            residual,
            [None] + [factors[0, j] for j in range(half)],
            [factors[1, j] for j in range(half)],
        )
        for j in range(half):
            solved[j] = local[j, f] + solved[j]
            base[j, f] = solved[j]
        message[pl.ds(pl.multiple_of(f * rows, rows), rows), :] = solved[half - 1]
        return carry

    lax.fori_loop(0, functionals, step, 0)


def coefficient_kernel(planes, halo, spread, spread_other, response, ends, halo_response):
    side, _ = position()
    layers = planes.shape[0] - 3
    half = layers // 2
    has_above, has_below = edge_flags()
    top_row = lax.broadcasted_iota(jnp.int32, halo.shape[1:], 0) == 0
    halo_live = jnp.where(top_row, has_above, has_below)

    def both(get):
        multiplier, inverse, kappa = chip_factors(get, side, layers)
        unit = unit_response(multiplier, inverse)
        multiplier_other, inverse_other, _ = chip_factors(get, 1 - side, layers)
        unit_other = unit_response(multiplier_other, inverse_other)
        mine, other = kappa * unit[half - 1], kappa * unit_other[half - 1]
        return multiplier, inverse, kappa, unit, unit_other, (mine, other, 1.0 / (1.0 - mine * other))

    _, _, kappa, unit, unit_other, corner = both(lambda k: halo[k])
    rows_halo = halo.shape[1]
    for i in range(3):
        ends[i + 3, 0:rows_halo] = corner[i] * halo_live if i == 2 else corner[i]
    for j in range(half):
        halo_response[0, j] = kappa * unit[j] * halo_live
        halo_response[1, j] = kappa * unit_other[j] * halo_live
    multiplier, inverse, kappa, unit, unit_other, corner = both(lambda k: planes[k])
    for i in range(3):
        ends[i] = corner[i]
    horiz = planes[layers + 2]
    mine = [kappa * unit[j] for j in range(half)]
    other = [kappa * unit_other[j] for j in range(half)]
    for j in range(half):
        response[j] = mine[j]
    for direction in (UP, DOWN, LEFT, RIGHT):
        source, total = [], jnp.zeros_like(horiz)
        for j in range(half):
            edges = (None, None)
            if direction in (UP, DOWN):
                edges = tuple(halo_response[i, j, direction : direction + 1, :] for i in range(2))
            source.append(horiz * moved(mine[j], direction, edges[0]))
            total = total + unit_other[j] * moved(other[j], direction, edges[1])
        spread_other[direction] = horiz * total
        for j, value in enumerate(chip_solve(source, multiplier, inverse)):
            spread[direction, j] = value


def interface_kernel(
    base, boundary, boundary_other, message_mine, message, spread, spread_other, ends, near, diag,
    around_all, second_all, sums, halo_mine, halo_other,
):
    half, functionals, rows, _ = base.shape
    last = functionals * (rows + 2)
    sums[...] = message_mine[last:, :] + message[last:, :]
    if near is not None:
        sums[...] = sums[...] + (near[...] + diag[...])
    for i in range(2):
        start = functionals * (rows + i)
        here = message_mine[start : start + functionals, :]
        mine, other, inverse = (ends[k, i : i + 1, :] for k in (3, 4, 5))
        live = jnp.where(inverse == 0.0, 0.0, 1.0)
        value = (message[start : start + functionals, :] + other * here) * inverse
        halo_other[i] = value
        halo_mine[i] = (here + mine * value) * live

    def step(f, carry):
        here = boundary[f]
        mine, other, inverse = ends[0], ends[1], ends[2]
        value = (boundary_other[f] + other * here) * inverse
        value_mine = here + mine * value

        def around(plane, edges):
            return [
                moved(plane, UP, edges[0, pl.ds(f, 1), :]),
                moved(plane, DOWN, edges[1, pl.ds(f, 1), :]),
                moved(plane, LEFT),
                moved(plane, RIGHT),
            ]

        value_around = around(value, halo_other)
        mine_around = around(value_mine, halo_mine)
        last = base[half - 1, f]
        last_other = message[pl.ds(pl.multiple_of(f * rows, rows), rows), :]
        for d in range(4):
            around_all[d, f] = value_around[d]
            last = last + spread[d, half - 1] * value_around[d]
            last_other = last_other + spread_other[d] * mine_around[d]
        second_all[f] = (last_other + other * last) * inverse
        return carry

    lax.fori_loop(0, functionals, step, 0)


def final_kernel(base, around_all, second_all, spread, response, out, *, other_core):
    side, core = position()
    half, functionals = base.shape[0], base.shape[1]
    held = half // 2
    group = 1 - core if other_core else core

    def step(f, carry):
        second = second_all[f]
        value_around = [around_all[d, f] for d in range(4)]
        for i in range(held):
            m = group * held + i
            j = jnp.where(side == 0, m, half - 1 - m)
            value = base[j, f] + response[j] * second
            for d in range(4):
                value = value + spread[d, j] * value_around[d]
            out[i, f] = value
        return carry

    lax.fori_loop(0, functionals, step, 0)


def call(
    kernel, out_shapes, scratch=(), any_inputs=(), hbm_inputs=(), any_outputs=(), aliases=None
):
    def run(*operands):
        spaces = [
            pltpu.HBM if i in hbm_inputs else pl.ANY if i in any_inputs else pltpu.VMEM
            for i in range(len(operands))
        ]
        in_specs = [pl.BlockSpec(memory_space=space) for space in spaces]
        operands = [
            pltpu.with_memory_space_constraint(x, pltpu.HBM) if space is pltpu.HBM else x
            for x, space in zip(operands, spaces)
        ]
        return pl.pallas_call(
            kernel,
            out_shape=[jax.ShapeDtypeStruct(s, jnp.float32) for s in out_shapes],
            in_specs=in_specs,
            out_specs=[
                pl.BlockSpec(memory_space=pl.ANY if i in any_outputs else pltpu.VMEM)
                for i in range(len(out_shapes))
            ],
            scratch_shapes=list(scratch),
            input_output_aliases=aliases or {},
            compiler_params=pltpu.CompilerParams(vmem_limit_bytes=VMEM_BYTES),
        )(*operands)

    return run


def add_parts(values, parts):
    values = values + parts[0]
    return values + (parts[1] + parts[2]) if len(parts) == 3 else values


def after(value, *earlier):
    return lax.optimization_barrier((value, *earlier))[0]


def shards(forcing, vert_coupling, horiz_coupling, basal_velocity, group_label, ice_mask):
    layers, rows, width_block = vert_coupling.shape
    held, functionals_all, _, width = forcing.shape
    half, functionals = layers // 2, functionals_all // 2
    tiles = lax.axis_size("tile")
    f32 = jnp.float32

    def send(array, target):
        pairs = []
        for t in range(tiles):
            for i in range(4):
                u, k = target(t, i)
                pairs.append((4 * t + i, 4 * u + k))
        return lax.ppermute(array, ("tile", "layer"), pairs)

    def across(array, bits):
        return send(array, lambda t, i: (t, i ^ bits))

    def parity(t):
        return bin(t).count("1") % 2

    def to_near(array, bits=None):
        return to_tile(array, bits, lambda t: t ^ 1)

    def to_far(array, bits=None):
        return to_tile(array, bits, lambda t: t + 1 if t % 2 else t - 1)

    def to_tile(array, bits, partner):
        def target(t, i):
            u = partner(t)
            if not 0 <= u < tiles:
                return t, i ^ 1
            return u, i ^ ((parity(t) + parity(u)) % 2 if bits is None else bits)

        return send(array, target)

    def exchange(values, masks):
        kinds = list(masks)
        if len(masks) == 2:
            kinds.append(masks[0] | masks[1])
        return [send(values, lambda t, i: (t ^ d, i ^ (n < 2))) for n, d in enumerate(kinds)]

    dma = pltpu.SemaphoreType.DMA
    count = layers + 3
    edge_rows = -(-count // 8) * 8
    stack = half * functionals
    flat = (rows, width_block)
    quarter = (held, functionals, rows, width)
    join = lax.optimization_barrier
    block, forcing_sent, forcing_kept = call(
        pack_kernel,
        [(layers + 2, *flat), quarter, quarter],
        [pltpu.VMEM(flat, f32), pltpu.VMEM(flat, jnp.int32), pltpu.VMEM(flat, jnp.int32), dma((6,))],
        hbm_inputs=range(5),
    )(vert_coupling, basal_velocity, group_label, ice_mask, forcing)
    cross, peer, forcing_received = join(
        (across(block, 3), across(block, 1), across(forcing_sent, 1))
    )
    diag = across(cross, 1)
    planes, edge_near, edge_far = call(
        assemble_kernel, [(count, rows, width), (edge_rows, width), (edge_rows, width)]
    )(block, peer, cross, diag, horiz_coupling)
    edge_far = to_far(edge_far, 1)
    edge_near = to_near(edge_near, 1)

    gathered = pltpu.VMEM((half, functionals, rows, width), f32)
    factors = pltpu.VMEM((2, half, rows, width), f32)
    columns_all = tiles * rows * width
    scale = -((columns_all / GROUPS) ** -0.5)
    (sums_inside,) = call(
        functools.partial(column_kernel, scale=scale),
        [(functionals, GROUPS)],
        [
            gathered,
            pltpu.VMEM((5, layers, rows, width), f32),
            pltpu.VMEM((functionals, rows, width), f32),
            dma((2,)),
        ],
        any_inputs=(0, 1),
    )(forcing_kept, forcing_received, planes)
    local, boundary, rows_near, rows_far = call(
        local_kernel,
        [(half, functionals, rows, width), (functionals, rows, width), (stack, width), (stack, width)],
        [gathered, factors, dma((2,))],
        any_inputs=(0, 1),
    )(forcing_kept, forcing_received, planes)
    rows_far, rows_near, boundary, edge_near, edge_far = join(
        (rows_far, rows_near, boundary, edge_near, edge_far)
    )
    rows_far = to_far(rows_far)
    rows_near = to_near(rows_near)
    boundary_other = across(boundary, 3)
    sums, halo = call(
        functools.partial(border_kernel, scale=scale),
        [(functionals, GROUPS), (count, 8, width)],
    )(forcing_kept, forcing_received, planes, edge_near, edge_far, sums_inside)

    spread, spread_other, response, ends = call(
        coefficient_kernel,
        [(4, half, rows, width), (4, rows, width), (half, rows, width), (6, rows, width)],
        [pltpu.VMEM((2, half, 8, width), f32)],
    )(planes, halo)

    masks = [1 << bit for bit in range(1, (tiles - 1).bit_length())]
    while len(masks) > 2:
        sums = add_parts(sums, exchange(sums, masks[:2]))
        masks = masks[2:]
    parts = exchange(sums, masks)
    base, message = call(
        middle_kernel,
        [(half, functionals, rows, width), (functionals * (rows + 3), width)],
        [factors],
    )(after(local, spread), planes, rows_near, rows_far)
    (message,) = call(
        fold_kernel,
        [message.shape],
        aliases={len(parts) + 1: 0},
    )(after(sums, boundary_other), *parts, message)
    message_other = across(message, 3)
    sums = message[functionals * (rows + 2) :]
    near = send(sums, lambda t, i: (t ^ 1, i ^ 1))
    diag = send(sums, lambda t, i: (t ^ 1, i ^ 2))
    message_other, near, diag = join((message_other, near, diag))
    halo_rows_both = pltpu.VMEM((2, functionals, width), f32)
    around, second, sums = call(
        interface_kernel,
        [(4, functionals, rows, width), (functionals, rows, width), (functionals, GROUPS)],
        [halo_rows_both, halo_rows_both],
    )(base, boundary, boundary_other, message, message_other, spread, spread_other, ends, near, diag)
    (sent,) = call(functools.partial(final_kernel, other_core=True), [quarter])(
        base, around, second, spread, response
    )
    (kept,) = call(functools.partial(final_kernel, other_core=False), [quarter])(
        base, around, second, spread, response
    )
    received, other_sums, kept = join((across(sent, 1), across(sums, 1), kept))
    adjoint, sums = call(
        place_kernel,
        [(held, functionals_all, rows, width), (functionals_all, GROUPS)],
        [dma((4,))],
        any_inputs=(0, 1, 2, 3),
        any_outputs=(0, 1),
    )(kept, received, sums, other_sums)
    return (adjoint, sums)


def solution(mesh):
    in_specs = (
        P("layer", None, "tile", None),
        P(None, "tile", "layer"),
        P("tile", None),
        P("tile", "layer"),
        P("tile", "layer"),
        P("tile", "layer"),
    )
    out_specs = (P("layer", None, "tile", None), P())
    return jax.shard_map(shards, mesh=mesh, in_specs=in_specs, out_specs=out_specs, check_vma=False)
```

```python
import functools

import jax
import jax.numpy as jnp
from jax import lax
from jax.experimental import pallas as pl
from jax.experimental.pallas import tpu as pltpu
from jax.sharding import PartitionSpec as P

GROUPS = 512
LANES = 128
VMEM_BYTES = 32 * 1024 * 1024
UP, DOWN, LEFT, RIGHT = range(4)


def position():
    layer = lax.axis_index("layer")
    return layer // 2, layer % 2


def owned_half():
    side, core = position()
    tile = lax.axis_index("tile")
    total = side + core
    for bit in range((lax.axis_size("tile") - 1).bit_length()):
        total = total + lax.shift_right_logical(tile, bit) % 2
    return total % 2


def edge_flags():
    tile = lax.axis_index("tile")
    last = lax.axis_size("tile") - 1
    return (
        jnp.where(tile > 0, 1.0, 0.0).astype(jnp.float32),
        jnp.where(tile < last, 1.0, 0.0).astype(jnp.float32),
    )


def paired_rows(first, last):
    even = lax.axis_index("tile") % 2 == 0
    return jnp.where(even, last, first), jnp.where(even, first, last)


def halo_rows(near, far):
    even = lax.axis_index("tile") % 2 == 0
    return jnp.where(even, far, near), jnp.where(even, near, far)


def moved(plane, direction, halo=None):
    rows, width = plane.shape
    axis = 0 if direction in (UP, DOWN) else 1
    size = plane.shape[axis]
    first = direction in (UP, LEFT)
    rolled = pltpu.roll(plane, 1 if first else size - 1, axis)
    at_edge = lax.broadcasted_iota(jnp.int32, plane.shape, axis) == (0 if first else size - 1)
    filler = jnp.zeros_like(plane) if halo is None else jnp.broadcast_to(halo, plane.shape)
    return jnp.where(at_edge, filler, rolled)


def chip_factors(planes, side, layers):
    half = layers // 2
    horiz = planes(layers + 2)

    def coupling(j):
        if j == 0:
            return planes(0) * jnp.where(side == 0, 1.0, 0.0)
        return planes(jnp.where(side == 0, j, layers - j))

    multiplier, inverse = [None], []
    below = coupling(0)
    for j in range(half):
        above = coupling(j + 1)
        pivot = below + above + 4.0 * horiz
        if j > 0:
            pivot = pivot - below * multiplier[j]
        inverse.append(1.0 / pivot)
        multiplier.append(above * inverse[j])
        below = above
    return multiplier, inverse, below


def unit_response(multiplier, inverse):
    half = len(inverse)
    response = [None] * half
    response[half - 1] = inverse[half - 1]
    for j in range(half - 2, -1, -1):
        response[j] = multiplier[j + 1] * response[j + 1]
    return response


def chip_solve(values, multiplier, inverse):
    half = len(values)
    swept = [values[0]]
    for j in range(1, half):
        swept.append(values[j] + multiplier[j] * swept[j - 1])
    solved = [None] * half
    solved[half - 1] = swept[half - 1] * inverse[half - 1]
    for j in range(half - 2, -1, -1):
        solved[j] = swept[j] * inverse[j] + multiplier[j + 1] * solved[j + 1]
    return solved


def pack_kernel(
    coupling, velocity, label, mask, forcing, block, sent, kept, velocity_in, label_in, mask_in, sems
):
    mine = owned_half()
    layers = coupling.shape[0]
    functionals = sent.shape[1]
    pairs = [
        (coupling, block.at[pl.ds(0, layers)]),
        (velocity, velocity_in),
        (label, label_in),
        (mask, mask_in),
    ]
    for target, which in ((sent, 1 - mine), (kept, mine)):
        pairs.append((forcing.at[:, pl.ds(which * functionals, functionals)], target))
    copies = [pltpu.make_async_copy(a, b, sems.at[i]) for i, (a, b) in enumerate(pairs)]
    for copy in copies:
        copy.start()
    for copy in copies[:4]:
        copy.wait()
    block[layers] = block[0] * velocity_in[...] * mask_in[...].astype(jnp.float32)
    block[layers + 1] = label_in[...].astype(jnp.float32)
    for copy in copies[4:]:
        copy.wait()


def rows_kernel(kept, received, row_near, row_far):
    _, core = position()
    held, functionals, rows, _ = kept.shape
    for source, first in ((kept, core * held), (received, (1 - core) * held)):
        for i in range(held):
            near, far = paired_rows(source[i, :, 0, :], source[i, :, rows - 1, :])
            at = pl.ds(pl.multiple_of((first + i) * functionals, functionals), functionals)
            row_near[at, :] = near
            row_far[at, :] = far


def place_kernel(kept, received, mine_sums, other_sums, out, sums, sems):
    mine = owned_half()
    functionals = kept.shape[1]
    copies = []
    for i, (source, group, which) in enumerate(((received, other_sums, 1 - mine), (kept, mine_sums, mine))):
        at = pl.ds(pl.multiple_of(which * functionals, functionals), functionals)
        copies.append(pltpu.make_async_copy(source, out.at[:, at], sems.at[2 * i]))
        copies.append(pltpu.make_async_copy(group, sums.at[at], sems.at[2 * i + 1]))
    for copy in copies:
        copy.start()
    for copy in copies:
        copy.wait()


def assemble_kernel(own, peer, cross, diag, horiz, planes, row_near, row_far):
    layer = lax.axis_index("layer")
    count, rows = own.shape[0], own.shape[1]
    for k, block in ((0, own), (1, peer), (3, cross), (2, diag)):
        start = pl.multiple_of(jnp.bitwise_xor(layer, k) * LANES, LANES)
        planes[0:count, :, pl.ds(start, LANES)] = block[...]
    planes[count] = horiz[...]
    for k in range(row_near.shape[0]):
        at = min(k, count)
        near, far = paired_rows(planes[at, 0:1, :], planes[at, rows - 1 : rows, :])
        row_near[k : k + 1, :] = near
        row_far[k : k + 1, :] = far


def load_forcing(own, received, gathered, sems):
    _, core = position()
    held = received.shape[0]
    copies = (
        pltpu.make_async_copy(own, gathered.at[pl.ds(core * held, held)], sems.at[0]),
        pltpu.make_async_copy(received, gathered.at[pl.ds((1 - core) * held, held)], sems.at[1]),
    )
    for copy in copies:
        copy.start()
    return copies


def local_kernel(own, received, planes, local, boundary, gathered, factors, sems):
    side, _ = position()
    copies = load_forcing(own, received, gathered, sems)
    layers = planes.shape[0] - 3
    half, functionals, rows, _ = local.shape
    multiplier, inverse, _ = chip_factors(lambda k: planes[k], side, layers)
    for j in range(half):
        factors[0, j] = multiplier[j + 1]
        factors[1, j] = inverse[j]
    for copy in copies:
        copy.wait()

    def step(f, carry):
        values = [gathered[side * (half - 1) + (1 - 2 * side) * j, f] for j in range(half)]
        solved = chip_solve(
            values,
            [None] + [factors[0, j] for j in range(half)],
            [factors[1, j] for j in range(half)],
        )
        for j in range(half):
            local[j, f] = solved[j]
        boundary[f] = solved[half - 1]
        return carry

    lax.fori_loop(0, functionals, step, 0)


def full_factors(get, layers):
    multiplier, inverse = [None], []
    horiz = get(layers + 2)
    low = get(0)
    for k in range(layers):
        high = get(k + 1) if k + 1 < layers else jnp.zeros_like(low)
        pivot = low + high + 4.0 * horiz
        if k > 0:
            pivot = pivot - low * multiplier[k]
        inverse.append(1.0 / pivot)
        multiplier.append(high * inverse[k])
        low = high
    return multiplier, inverse


def bed_row(multiplier, inverse):
    layers = len(inverse)
    swept = [jnp.ones_like(inverse[0])]
    for k in range(1, layers):
        swept.append(multiplier[k] * swept[k - 1])
    solved = [None] * layers
    solved[layers - 1] = swept[layers - 1] * inverse[layers - 1]
    for k in range(layers - 2, -1, -1):
        solved[k] = swept[k] * inverse[k] + multiplier[k + 1] * solved[k + 1]
    return solved


def grouped(values, labels):
    label = labels.astype(jnp.int32)
    parts = []
    for b in range(GROUPS // LANES):
        inside = jnp.broadcast_to((label // LANES) == b, values.shape)
        parts.append(jnp.where(inside, values, 0.0))
    left = jnp.concatenate(parts, axis=0)
    high = left.astype(jnp.bfloat16)
    rest = left - high.astype(jnp.float32)
    middle = rest.astype(jnp.bfloat16)
    low = (rest - middle.astype(jnp.float32)).astype(jnp.bfloat16)
    left = jnp.concatenate([high, middle, low], axis=0)
    place = lax.broadcasted_iota(jnp.int32, (LANES, values.shape[1]), 0)
    match = jnp.where(jnp.broadcast_to(label % LANES, place.shape) == place, 1.0, 0.0)
    return lax.dot_general(
        left,
        match.astype(jnp.bfloat16),
        (((1,), (1,)), ((), ())),
        preferred_element_type=jnp.float32,
    )


def add_groups(sums, total, scale, functionals):
    blocks = GROUPS // LANES
    size = blocks * functionals
    total = (total[0:size] + total[size : 2 * size] + total[2 * size :]) * scale
    for b in range(blocks):
        lanes = slice(b * LANES, (b + 1) * LANES)
        sums[:, lanes] = sums[:, lanes] + total[b * functionals : (b + 1) * functionals]


def column_kernel(own, received, planes, sums, gathered, weights, terms, sems, *, scale):
    side, core = position()
    copies = load_forcing(own, received, gathered, sems)
    layers = planes.shape[0] - 3
    half, functionals, rows, _ = gathered.shape
    multiplier, inverse = full_factors(lambda k: planes[k], layers)
    weight = planes[layers]
    spread = weight * planes[layers + 2]
    for k, value in enumerate(bed_row(multiplier, inverse)):
        weights[4, k] = value
    for direction in (UP, DOWN, LEFT, RIGHT):
        source = [moved(weights[4, k] * spread, direction) for k in range(layers)]
        for k, value in enumerate(chip_solve(source, multiplier, inverse)):
            weights[direction, k] = value
    for k in range(layers):
        weights[4, k] = weights[4, k] * weight
    for copy in copies:
        copy.wait()

    def step(f, carry):
        values = [gathered[m, f] for m in range(half)]

        def total(kind):
            out = values[0] * weights[kind, side * half]
            for m in range(1, half):
                out = out + values[m] * weights[kind, side * half + m]
            return out

        here = total(4) + moved(total(UP), DOWN) + moved(total(DOWN), UP)
        terms[f] = here + moved(total(LEFT), RIGHT) + moved(total(RIGHT), LEFT)
        return carry

    lax.fori_loop(0, functionals, step, 0)
    total = grouped(terms[:, 0, :], planes[layers + 1, 0:1, :])
    for y in range(1, rows):
        total = total + grouped(terms[:, y, :], planes[layers + 1, y : y + 1, :])
    sums[...] = jnp.zeros_like(sums)
    add_groups(sums, total, scale, functionals)


def border_kernel(own, received, planes, near, far, inside, sums, halo, *, scale):
    side, core = position()
    layers = planes.shape[0] - 3
    held, functionals, rows, width = received.shape
    top_row = lax.broadcasted_iota(jnp.int32, halo.shape[1:], 0) == 0
    has_above, has_below = edge_flags()

    def pair(above, below):
        return jnp.where(
            top_row, jnp.broadcast_to(above, halo.shape[1:]), jnp.broadcast_to(below, halo.shape[1:])
        )

    for k in range(layers + 3):
        halo[k] = pair(*halo_rows(near[k : k + 1, :], far[k : k + 1, :]))
    outer = bed_row(*full_factors(lambda k: halo[k], layers))
    live = halo[layers] * halo[layers + 2] * jnp.where(top_row, has_above, has_below)
    edge = full_factors(lambda k: pair(planes[k, 0:1, :], planes[k, rows - 1 : rows, :]), layers)
    solved = chip_solve([value * live for value in outer], *edge)
    sums[...] = inside[...]
    total = None
    for which, row in enumerate((0, rows - 1)):
        out = None
        for m in range(2 * held):
            weight = jnp.where(side == 0, solved[m][which : which + 1], solved[2 * held + m][which : which + 1])
            mine, other = own[m % held, :, row, :], received[m % held, :, row, :]
            value = jnp.where(core == m // held, mine, other) * weight
            out = value if out is None else out + value
        part = grouped(out, halo[layers + 1, which : which + 1, :])
        total = part if total is None else total + part
    add_groups(sums, total, scale, functionals)


def fold_kernel(mine, *refs):
    parts, message, out = refs[:-2], refs[-2], refs[-1]
    total = mine[...]
    if parts:
        total = total + parts[0][...]
    if len(parts) == 3:
        total = total + (parts[1][...] + parts[2][...])
    size = mine.shape[0]
    out[out.shape[0] - size :, :] = total


def middle_kernel(local, planes, halo, near, far, base, message, factors, outside):
    side, _ = position()
    layers = planes.shape[0] - 3
    half, functionals, rows, _ = local.shape
    multiplier, inverse, _ = chip_factors(lambda k: halo[k], side, layers)
    around = []
    for m in range(half):
        at = slice(m * functionals, (m + 1) * functionals)
        around.append(halo_rows(near[at, :], far[at, :]))
    for which, live in enumerate(edge_flags()):
        values = [
            jnp.where(side == 0, around[j][which], around[half - 1 - j][which]) for j in range(half)
        ]
        solved = chip_solve(
            values,
            [None] + [m[which : which + 1] for m in multiplier[1:]],
            [v[which : which + 1] for v in inverse],
        )
        for j in range(half):
            outside[which, j] = solved[j] * live
        start = functionals * (rows + which)
        message[start : start + functionals, :] = solved[half - 1]
    multiplier, inverse, _ = chip_factors(lambda k: planes[k], side, layers)
    for j in range(half):
        factors[0, j] = multiplier[j + 1]
        factors[1, j] = inverse[j]

    def step(f, carry):
        horiz = planes[layers + 2]
        residual = []
        for j in range(half):
            here = local[j, f]
            at = pl.ds(f, 1)
            around = moved(here, UP, outside[0, j, at, :]) + moved(here, DOWN, outside[1, j, at, :])
            around = around + moved(here, LEFT) + moved(here, RIGHT)
            residual.append(horiz * around)
        solved = chip_solve(
            residual,
            [None] + [factors[0, j] for j in range(half)],
            [factors[1, j] for j in range(half)],
        )
        for j in range(half):
            solved[j] = local[j, f] + solved[j]
            base[j, f] = solved[j]
        message[pl.ds(pl.multiple_of(f * rows, rows), rows), :] = solved[half - 1]
        return carry

    lax.fori_loop(0, functionals, step, 0)


def coefficient_kernel(planes, halo, spread, spread_other, response, ends, halo_response):
    side, _ = position()
    layers = planes.shape[0] - 3
    half = layers // 2
    has_above, has_below = edge_flags()
    top_row = lax.broadcasted_iota(jnp.int32, halo.shape[1:], 0) == 0
    halo_live = jnp.where(top_row, has_above, has_below)

    def both(get):
        multiplier, inverse, kappa = chip_factors(get, side, layers)
        unit = unit_response(multiplier, inverse)
        multiplier_other, inverse_other, _ = chip_factors(get, 1 - side, layers)
        unit_other = unit_response(multiplier_other, inverse_other)
        mine, other = kappa * unit[half - 1], kappa * unit_other[half - 1]
        return multiplier, inverse, kappa, unit, unit_other, (mine, other, 1.0 / (1.0 - mine * other))

    _, _, kappa, unit, unit_other, corner = both(lambda k: halo[k])
    rows_halo = halo.shape[1]
    for i in range(3):
        ends[i + 3, 0:rows_halo] = corner[i] * halo_live if i == 2 else corner[i]
    for j in range(half):
        halo_response[0, j] = kappa * unit[j] * halo_live
        halo_response[1, j] = kappa * unit_other[j] * halo_live
    multiplier, inverse, kappa, unit, unit_other, corner = both(lambda k: planes[k])
    for i in range(3):
        ends[i] = corner[i]
    horiz = planes[layers + 2]
    mine = [kappa * unit[j] for j in range(half)]
    other = [kappa * unit_other[j] for j in range(half)]
    for j in range(half):
        response[j] = mine[j]
    for direction in (UP, DOWN, LEFT, RIGHT):
        source, total = [], jnp.zeros_like(horiz)
        for j in range(half):
            edges = (None, None)
            if direction in (UP, DOWN):
                edges = tuple(halo_response[i, j, direction : direction + 1, :] for i in range(2))
            source.append(horiz * moved(mine[j], direction, edges[0]))
            total = total + unit_other[j] * moved(other[j], direction, edges[1])
        spread_other[direction] = horiz * total
        for j, value in enumerate(chip_solve(source, multiplier, inverse)):
            spread[direction, j] = value


def interface_kernel(
    base, boundary, boundary_other, message_mine, message, spread, spread_other, ends, near, diag,
    around_all, second_all, sums, halo_mine, halo_other,
):
    half, functionals, rows, _ = base.shape
    last = functionals * (rows + 2)
    sums[...] = message_mine[last:, :] + message[last:, :]
    if near is not None:
        sums[...] = sums[...] + (near[...] + diag[...])
    for i in range(2):
        start = functionals * (rows + i)
        here = message_mine[start : start + functionals, :]
        mine, other, inverse = (ends[k, i : i + 1, :] for k in (3, 4, 5))
        live = jnp.where(inverse == 0.0, 0.0, 1.0)
        value = (message[start : start + functionals, :] + other * here) * inverse
        halo_other[i] = value
        halo_mine[i] = (here + mine * value) * live

    def step(f, carry):
        here = boundary[f]
        mine, other, inverse = ends[0], ends[1], ends[2]
        value = (boundary_other[f] + other * here) * inverse
        value_mine = here + mine * value

        def around(plane, edges):
            return [
                moved(plane, UP, edges[0, pl.ds(f, 1), :]),
                moved(plane, DOWN, edges[1, pl.ds(f, 1), :]),
                moved(plane, LEFT),
                moved(plane, RIGHT),
            ]

        value_around = around(value, halo_other)
        mine_around = around(value_mine, halo_mine)
        last = base[half - 1, f]
        last_other = message[pl.ds(pl.multiple_of(f * rows, rows), rows), :]
        for d in range(4):
            around_all[d, f] = value_around[d]
            last = last + spread[d, half - 1] * value_around[d]
            last_other = last_other + spread_other[d] * mine_around[d]
        second_all[f] = (last_other + other * last) * inverse
        return carry

    lax.fori_loop(0, functionals, step, 0)


def final_kernel(base, around_all, second_all, spread, response, out, *, other_core):
    side, core = position()
    half, functionals = base.shape[0], base.shape[1]
    held = half // 2
    group = 1 - core if other_core else core

    def step(f, carry):
        second = second_all[f]
        value_around = [around_all[d, f] for d in range(4)]
        for i in range(held):
            m = group * held + i
            j = jnp.where(side == 0, m, half - 1 - m)
            value = base[j, f] + response[j] * second
            for d in range(4):
                value = value + spread[d, j] * value_around[d]
            out[i, f] = value
        return carry

    lax.fori_loop(0, functionals, step, 0)


def call(
    kernel, out_shapes, scratch=(), any_inputs=(), hbm_inputs=(), any_outputs=(), aliases=None
):
    def run(*operands):
        spaces = [
            pltpu.HBM if i in hbm_inputs else pl.ANY if i in any_inputs else pltpu.VMEM
            for i in range(len(operands))
        ]
        in_specs = [pl.BlockSpec(memory_space=space) for space in spaces]
        operands = [
            pltpu.with_memory_space_constraint(x, pltpu.HBM) if space is pltpu.HBM else x
            for x, space in zip(operands, spaces)
        ]
        return pl.pallas_call(
            kernel,
            out_shape=[jax.ShapeDtypeStruct(s, jnp.float32) for s in out_shapes],
            in_specs=in_specs,
            out_specs=[
                pl.BlockSpec(memory_space=pl.ANY if i in any_outputs else pltpu.VMEM)
                for i in range(len(out_shapes))
            ],
            scratch_shapes=list(scratch),
            input_output_aliases=aliases or {},
            compiler_params=pltpu.CompilerParams(vmem_limit_bytes=VMEM_BYTES),
        )(*operands)

    return run


def add_parts(values, parts):
    values = values + parts[0]
    return values + (parts[1] + parts[2]) if len(parts) == 3 else values


def after(value, *earlier):
    return lax.optimization_barrier((value, *earlier))[0]


def shards(forcing, vert_coupling, horiz_coupling, basal_velocity, group_label, ice_mask):
    layers, rows, width_block = vert_coupling.shape
    held, functionals_all, _, width = forcing.shape
    half, functionals = layers // 2, functionals_all // 2
    tiles = lax.axis_size("tile")
    f32 = jnp.float32

    def send(array, target):
        pairs = []
        for t in range(tiles):
            for i in range(4):
                u, k = target(t, i)
                pairs.append((4 * t + i, 4 * u + k))
        return lax.ppermute(array, ("tile", "layer"), pairs)

    def across(array, bits):
        return send(array, lambda t, i: (t, i ^ bits))

    def parity(t):
        return bin(t).count("1") % 2

    def to_near(array, bits=None):
        return to_tile(array, bits, lambda t: t ^ 1)

    def to_far(array, bits=None):
        return to_tile(array, bits, lambda t: t + 1 if t % 2 else t - 1)

    def to_tile(array, bits, partner):
        def target(t, i):
            u = partner(t)
            if not 0 <= u < tiles:
                return t, i ^ 1
            return u, i ^ ((parity(t) + parity(u)) % 2 if bits is None else bits)

        return send(array, target)

    def exchange(values, masks):
        kinds = list(masks)
        if len(masks) == 2:
            kinds.append(masks[0] | masks[1])
        return [send(values, lambda t, i: (t ^ d, i ^ (n < 2))) for n, d in enumerate(kinds)]

    dma = pltpu.SemaphoreType.DMA
    count = layers + 3
    edge_rows = -(-count // 8) * 8
    stack = half * functionals
    flat = (rows, width_block)
    quarter = (held, functionals, rows, width)
    join = lax.optimization_barrier
    block, forcing_sent, forcing_kept = call(
        pack_kernel,
        [(layers + 2, *flat), quarter, quarter],
        [pltpu.VMEM(flat, f32), pltpu.VMEM(flat, jnp.int32), pltpu.VMEM(flat, jnp.int32), dma((6,))],
        hbm_inputs=range(5),
    )(vert_coupling, basal_velocity, group_label, ice_mask, forcing)
    cross, peer, forcing_received = join(
        (across(block, 3), across(block, 1), across(forcing_sent, 1))
    )
    rows_near, rows_far = call(rows_kernel, [(stack, width), (stack, width)])(
        forcing_kept, forcing_received
    )
    rows_far = to_far(rows_far)
    rows_near = to_near(rows_near)
    diag = across(cross, 1)
    planes, edge_near, edge_far = call(
        assemble_kernel, [(count, rows, width), (edge_rows, width), (edge_rows, width)]
    )(block, peer, cross, diag, horiz_coupling)
    edge_far = to_far(edge_far, 1)
    edge_near = to_near(edge_near, 1)

    gathered = pltpu.VMEM((half, functionals, rows, width), f32)
    factors = pltpu.VMEM((2, half, rows, width), f32)
    columns_all = tiles * rows * width
    scale = -((columns_all / GROUPS) ** -0.5)
    (sums_inside,) = call(
        functools.partial(column_kernel, scale=scale),
        [(functionals, GROUPS)],
        [
            gathered,
            pltpu.VMEM((5, layers, rows, width), f32),
            pltpu.VMEM((functionals, rows, width), f32),
            dma((2,)),
        ],
        any_inputs=(0, 1),
    )(forcing_kept, forcing_received, planes)
    planes_later, edge_near, edge_far, sums_inside = join((planes, edge_near, edge_far, sums_inside))
    local, boundary = call(
        local_kernel,
        [(half, functionals, rows, width), (functionals, rows, width)],
        [gathered, factors, dma((2,))],
        any_inputs=(0, 1),
    )(forcing_kept, forcing_received, planes_later)
    sums, halo = call(
        functools.partial(border_kernel, scale=scale),
        [(functionals, GROUPS), (count, 8, width)],
    )(forcing_kept, forcing_received, planes, edge_near, edge_far, sums_inside)

    boundary_other = across(after(boundary, sums), 3)
    spread, spread_other, response, ends = call(
        coefficient_kernel,
        [(4, half, rows, width), (4, rows, width), (half, rows, width), (6, rows, width)],
        [pltpu.VMEM((2, half, 8, width), f32)],
    )(planes, halo)

    masks = [1 << bit for bit in range(1, (tiles - 1).bit_length())]
    while len(masks) > 2:
        sums = add_parts(sums, exchange(sums, masks[:2]))
        masks = masks[2:]
    parts = exchange(sums, masks)
    base, message = call(
        middle_kernel,
        [(half, functionals, rows, width), (functionals * (rows + 3), width)],
        [factors, pltpu.VMEM((2, half, functionals, width), f32)],
    )(after(local, spread), planes, halo, rows_near, rows_far)
    (message,) = call(
        fold_kernel,
        [message.shape],
        aliases={len(parts) + 1: 0},
    )(after(sums, boundary_other), *parts, message)
    message_other = across(message, 3)
    sums = message[functionals * (rows + 2) :]
    near = send(sums, lambda t, i: (t ^ 1, i ^ 1))
    diag = send(sums, lambda t, i: (t ^ 1, i ^ 2))
    message_other, near, diag = join((message_other, near, diag))
    halo_rows_both = pltpu.VMEM((2, functionals, width), f32)
    around, second, sums = call(
        interface_kernel,
        [(4, functionals, rows, width), (functionals, rows, width), (functionals, GROUPS)],
        [halo_rows_both, halo_rows_both],
    )(base, boundary, boundary_other, message, message_other, spread, spread_other, ends, near, diag)
    (sent,) = call(functools.partial(final_kernel, other_core=True), [quarter])(
        base, around, second, spread, response
    )
    (kept,) = call(functools.partial(final_kernel, other_core=False), [quarter])(
        base, around, second, spread, response
    )
    received, other_sums, kept = join((across(sent, 1), across(sums, 1), kept))
    adjoint, sums = call(
        place_kernel,
        [(held, functionals_all, rows, width), (functionals_all, GROUPS)],
        [dma((4,))],
        any_inputs=(0, 1, 2, 3),
        any_outputs=(0, 1),
    )(kept, received, sums, other_sums)
    return (adjoint, sums)


def solution(mesh):
    in_specs = (
        P("layer", None, "tile", None),
        P(None, "tile", "layer"),
        P("tile", None),
        P("tile", "layer"),
        P("tile", "layer"),
        P("tile", "layer"),
    )
    out_specs = (P("layer", None, "tile", None), P())
    return jax.shard_map(shards, mesh=mesh, in_specs=in_specs, out_specs=out_specs, check_vma=False)
```

```python
import functools

import jax
import jax.numpy as jnp
from jax import lax
from jax.experimental import pallas as pl
from jax.experimental.pallas import tpu as pltpu
from jax.sharding import PartitionSpec as P

GROUPS = 512
LANES = 128
VMEM_BYTES = 32 * 1024 * 1024
UP, DOWN, LEFT, RIGHT = range(4)


def position():
    layer = lax.axis_index("layer")
    return layer // 2, layer % 2


def owned_half():
    side, core = position()
    tile = lax.axis_index("tile")
    total = side + core
    for bit in range((lax.axis_size("tile") - 1).bit_length()):
        total = total + lax.shift_right_logical(tile, bit) % 2
    return total % 2


def edge_flags():
    tile = lax.axis_index("tile")
    last = lax.axis_size("tile") - 1
    return (
        jnp.where(tile > 0, 1.0, 0.0).astype(jnp.float32),
        jnp.where(tile < last, 1.0, 0.0).astype(jnp.float32),
    )


def paired_rows(first, last):
    even = lax.axis_index("tile") % 2 == 0
    return jnp.where(even, last, first), jnp.where(even, first, last)


def halo_rows(near, far):
    even = lax.axis_index("tile") % 2 == 0
    return jnp.where(even, far, near), jnp.where(even, near, far)


def moved(plane, direction, halo=None):
    rows, width = plane.shape
    axis = 0 if direction in (UP, DOWN) else 1
    size = plane.shape[axis]
    first = direction in (UP, LEFT)
    rolled = pltpu.roll(plane, 1 if first else size - 1, axis)
    at_edge = lax.broadcasted_iota(jnp.int32, plane.shape, axis) == (0 if first else size - 1)
    filler = jnp.zeros_like(plane) if halo is None else jnp.broadcast_to(halo, plane.shape)
    return jnp.where(at_edge, filler, rolled)


def chip_factors(planes, side, layers):
    half = layers // 2
    horiz = planes(layers + 2)

    def coupling(j):
        if j == 0:
            return planes(0) * jnp.where(side == 0, 1.0, 0.0)
        return planes(jnp.where(side == 0, j, layers - j))

    multiplier, inverse = [None], []
    below = coupling(0)
    for j in range(half):
        above = coupling(j + 1)
        pivot = below + above + 4.0 * horiz
        if j > 0:
            pivot = pivot - below * multiplier[j]
        inverse.append(1.0 / pivot)
        multiplier.append(above * inverse[j])
        below = above
    return multiplier, inverse, below


def unit_response(multiplier, inverse):
    half = len(inverse)
    response = [None] * half
    response[half - 1] = inverse[half - 1]
    for j in range(half - 2, -1, -1):
        response[j] = multiplier[j + 1] * response[j + 1]
    return response


def chip_solve(values, multiplier, inverse):
    half = len(values)
    swept = [values[0]]
    for j in range(1, half):
        swept.append(values[j] + multiplier[j] * swept[j - 1])
    solved = [None] * half
    solved[half - 1] = swept[half - 1] * inverse[half - 1]
    for j in range(half - 2, -1, -1):
        solved[j] = swept[j] * inverse[j] + multiplier[j + 1] * solved[j + 1]
    return solved


def pack_kernel(
    coupling, velocity, label, mask, forcing, block, sent, kept, velocity_in, label_in, mask_in, sems
):
    mine = owned_half()
    layers = coupling.shape[0]
    functionals = sent.shape[1]
    pairs = [
        (coupling, block.at[pl.ds(0, layers)]),
        (velocity, velocity_in),
        (label, label_in),
        (mask, mask_in),
    ]
    for target, which in ((sent, 1 - mine), (kept, mine)):
        pairs.append((forcing.at[:, pl.ds(which * functionals, functionals)], target))
    copies = [pltpu.make_async_copy(a, b, sems.at[i]) for i, (a, b) in enumerate(pairs)]
    for copy in copies:
        copy.start()
    for copy in copies[:4]:
        copy.wait()
    block[layers] = block[0] * velocity_in[...] * mask_in[...].astype(jnp.float32)
    block[layers + 1] = label_in[...].astype(jnp.float32)
    for copy in copies[4:]:
        copy.wait()


def rows_kernel(kept, received, row_near, row_far):
    _, core = position()
    held, functionals, rows, _ = kept.shape
    for source, first in ((kept, core * held), (received, (1 - core) * held)):
        for i in range(held):
            near, far = paired_rows(source[i, :, 0, :], source[i, :, rows - 1, :])
            at = pl.ds(pl.multiple_of((first + i) * functionals, functionals), functionals)
            row_near[at, :] = near
            row_far[at, :] = far


def place_kernel(kept, received, mine_sums, other_sums, out, sums, sems):
    mine = owned_half()
    functionals = kept.shape[1]
    copies = []
    for i, (source, group, which) in enumerate(((received, other_sums, 1 - mine), (kept, mine_sums, mine))):
        at = pl.ds(pl.multiple_of(which * functionals, functionals), functionals)
        copies.append(pltpu.make_async_copy(source, out.at[:, at], sems.at[2 * i]))
        copies.append(pltpu.make_async_copy(group, sums.at[at], sems.at[2 * i + 1]))
    for copy in copies:
        copy.start()
    for copy in copies:
        copy.wait()


def assemble_kernel(own, peer, cross, diag, horiz, planes, row_near, row_far):
    layer = lax.axis_index("layer")
    count, rows = own.shape[0], own.shape[1]
    for k, block in ((0, own), (1, peer), (3, cross), (2, diag)):
        start = pl.multiple_of(jnp.bitwise_xor(layer, k) * LANES, LANES)
        planes[0:count, :, pl.ds(start, LANES)] = block[...]
    planes[count] = horiz[...]
    for k in range(row_near.shape[0]):
        at = min(k, count)
        near, far = paired_rows(planes[at, 0:1, :], planes[at, rows - 1 : rows, :])
        row_near[k : k + 1, :] = near
        row_far[k : k + 1, :] = far


def local_kernel(own, received, planes, local, boundary, factors):
    side, core = position()
    layers = planes.shape[0] - 3
    half, functionals, rows, _ = local.shape
    held = half // 2
    multiplier, inverse, _ = chip_factors(lambda k: planes[k], side, layers)
    for j in range(half):
        factors[0, j] = multiplier[j + 1]
        factors[1, j] = inverse[j]

    def sweep(at_side, at_core):
        order = range(half) if at_side == 0 else range(half - 1, -1, -1)

        def step(f, carry):
            values = [(own if m // held == at_core else received)[m % held, f] for m in order]
            solved = chip_solve(
                values,
                [None] + [factors[0, j] for j in range(half)],
                [factors[1, j] for j in range(half)],
            )
            for j in range(half):
                local[j, f] = solved[j]
            boundary[f] = solved[half - 1]
            return carry

        lax.fori_loop(0, functionals, step, 0, unroll=8)

    for at_side in range(2):
        for at_core in range(2):
            pl.when((side == at_side) & (core == at_core))(
                functools.partial(sweep, at_side, at_core)
            )


def full_factors(get, layers):
    multiplier, inverse = [None], []
    horiz = get(layers + 2)
    low = get(0)
    for k in range(layers):
        high = get(k + 1) if k + 1 < layers else jnp.zeros_like(low)
        pivot = low + high + 4.0 * horiz
        if k > 0:
            pivot = pivot - low * multiplier[k]
        inverse.append(1.0 / pivot)
        multiplier.append(high * inverse[k])
        low = high
    return multiplier, inverse


def bed_row(multiplier, inverse):
    layers = len(inverse)
    swept = [jnp.ones_like(inverse[0])]
    for k in range(1, layers):
        swept.append(multiplier[k] * swept[k - 1])
    solved = [None] * layers
    solved[layers - 1] = swept[layers - 1] * inverse[layers - 1]
    for k in range(layers - 2, -1, -1):
        solved[k] = swept[k] * inverse[k] + multiplier[k + 1] * solved[k + 1]
    return solved


def grouped(values, labels):
    label = labels.astype(jnp.int32)
    parts = []
    for b in range(GROUPS // LANES):
        inside = jnp.broadcast_to((label // LANES) == b, values.shape)
        parts.append(jnp.where(inside, values, 0.0))
    left = jnp.concatenate(parts, axis=0)
    high = left.astype(jnp.bfloat16)
    rest = left - high.astype(jnp.float32)
    middle = rest.astype(jnp.bfloat16)
    low = (rest - middle.astype(jnp.float32)).astype(jnp.bfloat16)
    left = jnp.concatenate([high, middle, low], axis=0)
    place = lax.broadcasted_iota(jnp.int32, (LANES, values.shape[1]), 0)
    match = jnp.where(jnp.broadcast_to(label % LANES, place.shape) == place, 1.0, 0.0)
    return lax.dot_general(
        left,
        match.astype(jnp.bfloat16),
        (((1,), (1,)), ((), ())),
        preferred_element_type=jnp.float32,
    )


def add_groups(sums, total, scale, functionals):
    blocks = GROUPS // LANES
    size = blocks * functionals
    total = (total[0:size] + total[size : 2 * size] + total[2 * size :]) * scale
    for b in range(blocks):
        lanes = slice(b * LANES, (b + 1) * LANES)
        sums[:, lanes] = sums[:, lanes] + total[b * functionals : (b + 1) * functionals]


def column_kernel(own, received, planes, sums, weights, parts, terms, *, scale):
    side, core = position()
    layers = planes.shape[0] - 3
    held, functionals, rows, width = own.shape
    half = 2 * held
    multiplier, inverse = full_factors(lambda k: planes[k], layers)
    weight = planes[layers]
    spread = weight * planes[layers + 2]
    for k, value in enumerate(bed_row(multiplier, inverse)):
        weights[4, k] = value
    for direction in (UP, DOWN, LEFT, RIGHT):
        source = [moved(weights[4, k] * spread, direction) for k in range(layers)]
        for k, value in enumerate(chip_solve(source, multiplier, inverse)):
            weights[direction, k] = value
    for k in range(layers):
        weights[4, k] = weights[4, k] * weight

    def chunk(n, carry):
        lanes = pl.ds(pl.multiple_of(n * LANES, LANES), LANES)
        totals = [[None] * functionals for _ in range(5)]
        for source, first in ((own, core * held), (received, (1 - core) * held)):
            for i in range(held):
                factor = [weights[kind, side * half + first + i, :, lanes] for kind in range(5)]
                for f in range(functionals):
                    value = source[i, f, :, lanes]
                    for kind in range(5):
                        term = value * factor[kind]
                        old = totals[kind][f]
                        totals[kind][f] = term if old is None else old + term
        for kind in range(5):
            for f in range(functionals):
                parts[kind, f, :, lanes] = totals[kind][f]
        return carry

    lax.fori_loop(0, width // LANES, chunk, 0, unroll=4)

    def step(f, carry):
        here = parts[4, f] + moved(parts[UP, f], DOWN) + moved(parts[DOWN, f], UP)
        terms[f] = here + moved(parts[LEFT, f], RIGHT) + moved(parts[RIGHT, f], LEFT)
        return carry

    lax.fori_loop(0, functionals, step, 0, unroll=8)
    total = grouped(terms[:, 0, :], planes[layers + 1, 0:1, :])
    for y in range(1, rows):
        total = total + grouped(terms[:, y, :], planes[layers + 1, y : y + 1, :])
    sums[...] = jnp.zeros_like(sums)
    add_groups(sums, total, scale, functionals)


def border_kernel(local, planes, near, far, inside, sums, halo, *, scale):
    side, _ = position()
    layers = planes.shape[0] - 3
    half, functionals, rows, _ = local.shape
    top_row = lax.broadcasted_iota(jnp.int32, halo.shape[1:], 0) == 0
    has_above, has_below = edge_flags()

    def pair(above, below):
        return jnp.where(
            top_row, jnp.broadcast_to(above, halo.shape[1:]), jnp.broadcast_to(below, halo.shape[1:])
        )

    for k in range(layers + 3):
        halo[k] = pair(*halo_rows(near[k : k + 1, :], far[k : k + 1, :]))
    live = halo[layers] * halo[layers + 2] * jnp.where(top_row, has_above, has_below)
    lower, lower_inverse, kappa = chip_factors(lambda k: halo[k], 0, layers)
    upper, upper_inverse, _ = chip_factors(lambda k: halo[k], 1, layers)
    lower_unit, upper_unit = unit_response(lower, lower_inverse), unit_response(upper, upper_inverse)
    bed = chip_solve(
        [jnp.ones_like(kappa)] + [jnp.zeros_like(kappa)] * (half - 1), lower, lower_inverse
    )
    below_top = kappa * bed[half - 1] / (1.0 - kappa * lower_unit[half - 1] * kappa * upper_unit[half - 1])
    above_top = kappa * upper_unit[half - 1] * below_top
    lower_row = [live * (bed[j] + lower_unit[j] * above_top) for j in range(half)]
    upper_row = [live * (upper_unit[j] * below_top) for j in range(half)]
    mine = [jnp.where(side == 0, a, b) for a, b in zip(lower_row, upper_row)]
    other = [jnp.where(side == 0, b, a) for a, b in zip(lower_row, upper_row)]

    def edge(k):
        return pair(planes[k, 0:1, :], planes[k, rows - 1 : rows, :])

    multiplier, inverse, kappa = chip_factors(edge, side, layers)
    unit = unit_response(multiplier, inverse)
    unit_other = unit_response(*chip_factors(edge, 1 - side, layers)[:2])
    reach, reach_other = unit[0] * mine[0], unit_other[0] * other[0]
    for j in range(1, half):
        reach = reach + unit[j] * mine[j]
        reach_other = reach_other + unit_other[j] * other[j]
    far_side = kappa * unit_other[half - 1]
    across = (reach_other + far_side * reach) / (1.0 - kappa * unit[half - 1] * far_side)
    mine[half - 1] = mine[half - 1] + kappa * across
    sums[...] = inside[...]
    total = None
    for which, row in enumerate((0, rows - 1)):
        out = local[0, :, row, :] * mine[0][which : which + 1]
        for j in range(1, half):
            out = out + local[j, :, row, :] * mine[j][which : which + 1]
        part = grouped(out, halo[layers + 1, which : which + 1, :])
        total = part if total is None else total + part
    add_groups(sums, total, scale, functionals)


def fold_kernel(mine, *refs):
    parts, message, out = refs[:-2], refs[-2], refs[-1]
    total = mine[...]
    if parts:
        total = total + parts[0][...]
    if len(parts) == 3:
        total = total + (parts[1][...] + parts[2][...])
    size = mine.shape[0]
    out[out.shape[0] - size :, :] = total


def middle_kernel(local, planes, halo, near, far, base, message, factors, outside):
    side, _ = position()
    layers = planes.shape[0] - 3
    half, functionals, rows, _ = local.shape
    multiplier, inverse, _ = chip_factors(lambda k: halo[k], side, layers)
    around = []
    for m in range(half):
        at = slice(m * functionals, (m + 1) * functionals)
        around.append(halo_rows(near[at, :], far[at, :]))
    for which, live in enumerate(edge_flags()):
        values = [
            jnp.where(side == 0, around[j][which], around[half - 1 - j][which]) for j in range(half)
        ]
        solved = chip_solve(
            values,
            [None] + [m[which : which + 1] for m in multiplier[1:]],
            [v[which : which + 1] for v in inverse],
        )
        for j in range(half):
            outside[which, j] = solved[j] * live
        start = functionals * (rows + which)
        message[start : start + functionals, :] = solved[half - 1]
    multiplier, inverse, _ = chip_factors(lambda k: planes[k], side, layers)
    for j in range(half):
        factors[0, j] = multiplier[j + 1]
        factors[1, j] = inverse[j]

    def step(f, carry):
        horiz = planes[layers + 2]
        residual = []
        for j in range(half):
            here = local[j, f]
            at = pl.ds(f, 1)
            around = moved(here, UP, outside[0, j, at, :]) + moved(here, DOWN, outside[1, j, at, :])
            around = around + moved(here, LEFT) + moved(here, RIGHT)
            residual.append(horiz * around)
        solved = chip_solve(
            residual,
            [None] + [factors[0, j] for j in range(half)],
            [factors[1, j] for j in range(half)],
        )
        for j in range(half):
            solved[j] = local[j, f] + solved[j]
            base[j, f] = solved[j]
        message[pl.ds(pl.multiple_of(f * rows, rows), rows), :] = solved[half - 1]
        return carry

    lax.fori_loop(0, functionals, step, 0, unroll=8)


def coefficient_kernel(planes, halo, spread, spread_other, response, ends, halo_response):
    side, _ = position()
    layers = planes.shape[0] - 3
    half = layers // 2
    has_above, has_below = edge_flags()
    top_row = lax.broadcasted_iota(jnp.int32, halo.shape[1:], 0) == 0
    halo_live = jnp.where(top_row, has_above, has_below)

    def both(get):
        multiplier, inverse, kappa = chip_factors(get, side, layers)
        unit = unit_response(multiplier, inverse)
        multiplier_other, inverse_other, _ = chip_factors(get, 1 - side, layers)
        unit_other = unit_response(multiplier_other, inverse_other)
        mine, other = kappa * unit[half - 1], kappa * unit_other[half - 1]
        return multiplier, inverse, kappa, unit, unit_other, (mine, other, 1.0 / (1.0 - mine * other))

    _, _, kappa, unit, unit_other, corner = both(lambda k: halo[k])
    rows_halo = halo.shape[1]
    for i in range(3):
        ends[i + 3, 0:rows_halo] = corner[i] * halo_live if i == 2 else corner[i]
    for j in range(half):
        halo_response[0, j] = kappa * unit[j] * halo_live
        halo_response[1, j] = kappa * unit_other[j] * halo_live
    multiplier, inverse, kappa, unit, unit_other, corner = both(lambda k: planes[k])
    for i in range(3):
        ends[i] = corner[i]
    horiz = planes[layers + 2]
    mine = [kappa * unit[j] for j in range(half)]
    other = [kappa * unit_other[j] for j in range(half)]
    for j in range(half):
        response[j] = mine[j]
    for direction in (UP, DOWN, LEFT, RIGHT):
        source, total = [], jnp.zeros_like(horiz)
        for j in range(half):
            edges = (None, None)
            if direction in (UP, DOWN):
                edges = tuple(halo_response[i, j, direction : direction + 1, :] for i in range(2))
            source.append(horiz * moved(mine[j], direction, edges[0]))
            total = total + unit_other[j] * moved(other[j], direction, edges[1])
        spread_other[direction] = horiz * total
        for j, value in enumerate(chip_solve(source, multiplier, inverse)):
            spread[direction, j] = value


def interface_kernel(
    base, boundary, boundary_other, message_mine, message, spread, spread_other, ends, near, diag,
    around_all, second_all, sums, halo_mine, halo_other,
):
    half, functionals, rows, _ = base.shape
    last = functionals * (rows + 2)
    sums[...] = message_mine[last:, :] + message[last:, :]
    if near is not None:
        sums[...] = sums[...] + (near[...] + diag[...])
    for i in range(2):
        start = functionals * (rows + i)
        here = message_mine[start : start + functionals, :]
        mine, other, inverse = (ends[k, i : i + 1, :] for k in (3, 4, 5))
        live = jnp.where(inverse == 0.0, 0.0, 1.0)
        value = (message[start : start + functionals, :] + other * here) * inverse
        halo_other[i] = value
        halo_mine[i] = (here + mine * value) * live

    def step(f, carry):
        here = boundary[f]
        mine, other, inverse = ends[0], ends[1], ends[2]
        value = (boundary_other[f] + other * here) * inverse
        value_mine = here + mine * value

        def around(plane, edges):
            return [
                moved(plane, UP, edges[0, pl.ds(f, 1), :]),
                moved(plane, DOWN, edges[1, pl.ds(f, 1), :]),
                moved(plane, LEFT),
                moved(plane, RIGHT),
            ]

        value_around = around(value, halo_other)
        mine_around = around(value_mine, halo_mine)
        last = base[half - 1, f]
        last_other = message[pl.ds(pl.multiple_of(f * rows, rows), rows), :]
        for d in range(4):
            around_all[d, f] = value_around[d]
            last = last + spread[d, half - 1] * value_around[d]
            last_other = last_other + spread_other[d] * mine_around[d]
        second_all[f] = (last_other + other * last) * inverse
        return carry

    lax.fori_loop(0, functionals, step, 0, unroll=8)


def final_kernel(base, around_all, second_all, spread, response, out, *, other_core):
    side, core = position()
    half, functionals = base.shape[0], base.shape[1]
    held = half // 2
    group = 1 - core if other_core else core

    def step(f, carry):
        second = second_all[f]
        value_around = [around_all[d, f] for d in range(4)]
        for i in range(held):
            m = group * held + i
            j = jnp.where(side == 0, m, half - 1 - m)
            value = base[j, f] + response[j] * second
            for d in range(4):
                value = value + spread[d, j] * value_around[d]
            out[i, f] = value
        return carry

    lax.fori_loop(0, functionals, step, 0, unroll=8)


def call(
    kernel, out_shapes, scratch=(), any_inputs=(), hbm_inputs=(), any_outputs=(), aliases=None
):
    def run(*operands):
        spaces = [
            pltpu.HBM if i in hbm_inputs else pl.ANY if i in any_inputs else pltpu.VMEM
            for i in range(len(operands))
        ]
        in_specs = [pl.BlockSpec(memory_space=space) for space in spaces]
        operands = [
            pltpu.with_memory_space_constraint(x, pltpu.HBM) if space is pltpu.HBM else x
            for x, space in zip(operands, spaces)
        ]
        return pl.pallas_call(
            kernel,
            out_shape=[jax.ShapeDtypeStruct(s, jnp.float32) for s in out_shapes],
            in_specs=in_specs,
            out_specs=[
                pl.BlockSpec(memory_space=pl.ANY if i in any_outputs else pltpu.VMEM)
                for i in range(len(out_shapes))
            ],
            scratch_shapes=list(scratch),
            input_output_aliases=aliases or {},
            compiler_params=pltpu.CompilerParams(vmem_limit_bytes=VMEM_BYTES),
        )(*operands)

    return run


def add_parts(values, parts):
    values = values + parts[0]
    return values + (parts[1] + parts[2]) if len(parts) == 3 else values


def after(value, *earlier):
    return lax.optimization_barrier((value, *earlier))[0]


def shards(forcing, vert_coupling, horiz_coupling, basal_velocity, group_label, ice_mask):
    layers, rows, width_block = vert_coupling.shape
    held, functionals_all, _, width = forcing.shape
    half, functionals = layers // 2, functionals_all // 2
    tiles = lax.axis_size("tile")
    f32 = jnp.float32

    def send(array, target):
        pairs = []
        for t in range(tiles):
            for i in range(4):
                u, k = target(t, i)
                pairs.append((4 * t + i, 4 * u + k))
        return lax.ppermute(array, ("tile", "layer"), pairs)

    def across(array, bits):
        return send(array, lambda t, i: (t, i ^ bits))

    def parity(t):
        return bin(t).count("1") % 2

    def to_near(array, bits=None):
        return to_tile(array, bits, lambda t: t ^ 1)

    def to_far(array, bits=None):
        return to_tile(array, bits, lambda t: t + 1 if t % 2 else t - 1)

    def to_tile(array, bits, partner):
        def target(t, i):
            u = partner(t)
            if not 0 <= u < tiles:
                return t, i ^ 1
            return u, i ^ ((parity(t) + parity(u)) % 2 if bits is None else bits)

        return send(array, target)

    def exchange(values, masks):
        kinds = list(masks)
        if len(masks) == 2:
            kinds.append(masks[0] | masks[1])
        return [send(values, lambda t, i: (t ^ d, i ^ (n < 2))) for n, d in enumerate(kinds)]

    dma = pltpu.SemaphoreType.DMA
    count = layers + 3
    edge_rows = -(-count // 8) * 8
    stack = half * functionals
    flat = (rows, width_block)
    quarter = (held, functionals, rows, width)
    join = lax.optimization_barrier
    block, forcing_sent, forcing_kept = call(
        pack_kernel,
        [(layers + 2, *flat), quarter, quarter],
        [pltpu.VMEM(flat, f32), pltpu.VMEM(flat, jnp.int32), pltpu.VMEM(flat, jnp.int32), dma((6,))],
        hbm_inputs=range(5),
    )(vert_coupling, basal_velocity, group_label, ice_mask, forcing)
    cross, peer, forcing_received = join(
        (across(block, 3), across(block, 1), across(forcing_sent, 1))
    )
    rows_near, rows_far = call(rows_kernel, [(stack, width), (stack, width)])(
        forcing_kept, forcing_received
    )
    rows_far = to_far(rows_far)
    rows_near = to_near(rows_near)
    diag = across(cross, 1)
    planes, edge_near, edge_far = call(
        assemble_kernel, [(count, rows, width), (edge_rows, width), (edge_rows, width)]
    )(block, peer, cross, diag, horiz_coupling)
    edge_far = to_far(edge_far, 1)
    edge_near = to_near(edge_near, 1)

    factors = pltpu.VMEM((2, half, rows, width), f32)
    columns_all = tiles * rows * width
    scale = -((columns_all / GROUPS) ** -0.5)
    (sums_inside,) = call(
        functools.partial(column_kernel, scale=scale),
        [(functionals, GROUPS)],
        [
            pltpu.VMEM((5, layers, rows, width), f32),
            pltpu.VMEM((5, functionals, rows, width), f32),
            pltpu.VMEM((functionals, rows, width), f32),
        ],
    )(forcing_kept, forcing_received, planes)
    planes_later, edge_near, edge_far, sums_inside = join((planes, edge_near, edge_far, sums_inside))
    local, boundary = call(
        local_kernel,
        [(half, functionals, rows, width), (functionals, rows, width)],
        [factors],
    )(forcing_kept, forcing_received, planes)
    sums, halo = call(
        functools.partial(border_kernel, scale=scale),
        [(functionals, GROUPS), (count, 8, width)],
    )(local, planes, edge_near, edge_far, sums_inside)

    boundary_other = across(after(boundary, sums_inside), 3)
    spread, spread_other, response, ends = call(
        coefficient_kernel,
        [(4, half, rows, width), (4, rows, width), (half, rows, width), (6, rows, width)],
        [pltpu.VMEM((2, half, 8, width), f32)],
    )(planes, halo)

    masks = [1 << bit for bit in range(1, (tiles - 1).bit_length())]
    while len(masks) > 2:
        sums = add_parts(sums, exchange(sums, masks[:2]))
        masks = masks[2:]
    parts = exchange(sums, masks)
    base, message = call(
        middle_kernel,
        [(half, functionals, rows, width), (functionals * (rows + 3), width)],
        [factors, pltpu.VMEM((2, half, functionals, width), f32)],
    )(after(local, spread), planes, halo, rows_near, rows_far)
    (message,) = call(
        fold_kernel,
        [message.shape],
        aliases={len(parts) + 1: 0},
    )(after(sums, boundary_other), *parts, message)
    message_other = across(message, 3)
    sums = message[functionals * (rows + 2) :]
    near = send(sums, lambda t, i: (t ^ 1, i ^ 1))
    diag = send(sums, lambda t, i: (t ^ 1, i ^ 2))
    message_other, near, diag = join((message_other, near, diag))
    halo_rows_both = pltpu.VMEM((2, functionals, width), f32)
    around, second, sums = call(
        interface_kernel,
        [(4, functionals, rows, width), (functionals, rows, width), (functionals, GROUPS)],
        [halo_rows_both, halo_rows_both],
    )(base, boundary, boundary_other, message, message_other, spread, spread_other, ends, near, diag)
    (sent,) = call(functools.partial(final_kernel, other_core=True), [quarter])(
        base, around, second, spread, response
    )
    (kept,) = call(functools.partial(final_kernel, other_core=False), [quarter])(
        base, around, second, spread, response
    )
    received, other_sums, kept = join((across(sent, 1), across(sums, 1), kept))
    adjoint, sums = call(
        place_kernel,
        [(held, functionals_all, rows, width), (functionals_all, GROUPS)],
        [dma((4,))],
        any_inputs=(0, 1, 2, 3),
        any_outputs=(0, 1),
    )(kept, received, sums, other_sums)
    return (adjoint, sums)


def solution(mesh):
    in_specs = (
        P("layer", None, "tile", None),
        P(None, "tile", "layer"),
        P("tile", None),
        P("tile", "layer"),
        P("tile", "layer"),
        P("tile", "layer"),
    )
    out_specs = (P("layer", None, "tile", None), P())
    return jax.shard_map(shards, mesh=mesh, in_specs=in_specs, out_specs=out_specs, check_vma=False)
```

```python
import functools

import jax
import jax.numpy as jnp
from jax import lax
from jax.experimental import pallas as pl
from jax.experimental.pallas import tpu as pltpu
from jax.sharding import PartitionSpec as P

GROUPS = 512
LANES = 128
VMEM_BYTES = 32 * 1024 * 1024
UP, DOWN, LEFT, RIGHT = range(4)


def position():
    layer = lax.axis_index("layer")
    return layer // 2, layer % 2


def owned_half():
    side, core = position()
    tile = lax.axis_index("tile")
    total = side + core
    for bit in range((lax.axis_size("tile") - 1).bit_length()):
        total = total + lax.shift_right_logical(tile, bit) % 2
    return total % 2


def edge_flags():
    tile = lax.axis_index("tile")
    last = lax.axis_size("tile") - 1
    return (
        jnp.where(tile > 0, 1.0, 0.0).astype(jnp.float32),
        jnp.where(tile < last, 1.0, 0.0).astype(jnp.float32),
    )


def paired_rows(first, last):
    even = lax.axis_index("tile") % 2 == 0
    return jnp.where(even, last, first), jnp.where(even, first, last)


def halo_rows(near, far):
    even = lax.axis_index("tile") % 2 == 0
    return jnp.where(even, far, near), jnp.where(even, near, far)


def moved(plane, direction, halo=None):
    rows, width = plane.shape
    axis = 0 if direction in (UP, DOWN) else 1
    size = plane.shape[axis]
    first = direction in (UP, LEFT)
    rolled = pltpu.roll(plane, 1 if first else size - 1, axis)
    at_edge = lax.broadcasted_iota(jnp.int32, plane.shape, axis) == (0 if first else size - 1)
    filler = jnp.zeros_like(plane) if halo is None else jnp.broadcast_to(halo, plane.shape)
    return jnp.where(at_edge, filler, rolled)


def chip_factors(planes, side, layers):
    half = layers // 2
    horiz = planes(layers + 2)

    def coupling(j):
        if j == 0:
            return planes(0) * jnp.where(side == 0, 1.0, 0.0)
        return planes(jnp.where(side == 0, j, layers - j))

    multiplier, inverse = [None], []
    below = coupling(0)
    for j in range(half):
        above = coupling(j + 1)
        pivot = below + above + 4.0 * horiz
        if j > 0:
            pivot = pivot - below * multiplier[j]
        inverse.append(1.0 / pivot)
        multiplier.append(above * inverse[j])
        below = above
    return multiplier, inverse, below


def unit_response(multiplier, inverse):
    half = len(inverse)
    response = [None] * half
    response[half - 1] = inverse[half - 1]
    for j in range(half - 2, -1, -1):
        response[j] = multiplier[j + 1] * response[j + 1]
    return response


def chip_solve(values, multiplier, inverse):
    half = len(values)
    swept = [values[0]]
    for j in range(1, half):
        swept.append(values[j] + multiplier[j] * swept[j - 1])
    solved = [None] * half
    solved[half - 1] = swept[half - 1] * inverse[half - 1]
    for j in range(half - 2, -1, -1):
        solved[j] = swept[j] * inverse[j] + multiplier[j + 1] * solved[j + 1]
    return solved


def pack_kernel(
    coupling, velocity, label, mask, forcing, block, sent, kept, velocity_in, label_in, mask_in, sems
):
    mine = owned_half()
    layers = coupling.shape[0]
    functionals = sent.shape[1]
    pairs = [
        (coupling, block.at[pl.ds(0, layers)]),
        (velocity, velocity_in),
        (label, label_in),
        (mask, mask_in),
    ]
    for target, which in ((sent, 1 - mine), (kept, mine)):
        pairs.append((forcing.at[:, pl.ds(which * functionals, functionals)], target))
    copies = [pltpu.make_async_copy(a, b, sems.at[i]) for i, (a, b) in enumerate(pairs)]
    for copy in copies:
        copy.start()
    for copy in copies[:4]:
        copy.wait()
    block[layers] = block[0] * velocity_in[...] * mask_in[...].astype(jnp.float32)
    block[layers + 1] = label_in[...].astype(jnp.float32)
    for copy in copies[4:]:
        copy.wait()


def rows_kernel(kept, received, row_near, row_far):
    _, core = position()
    held, functionals, rows, _ = kept.shape
    for source, first in ((kept, core * held), (received, (1 - core) * held)):
        for i in range(held):
            near, far = paired_rows(source[i, :, 0, :], source[i, :, rows - 1, :])
            at = pl.ds(pl.multiple_of((first + i) * functionals, functionals), functionals)
            row_near[at, :] = near
            row_far[at, :] = far


def place_kept_kernel(kept, out, sem):
    functionals = kept.shape[1]
    at = pl.ds(pl.multiple_of(owned_half() * functionals, functionals), functionals)
    copy = pltpu.make_async_copy(kept, out.at[:, at], sem)
    copy.start()
    copy.wait()


def place_kernel(partly, received, mine_sums, other_sums, out, sums, sems):
    mine = owned_half()
    functionals = received.shape[1]
    at, other = (
        pl.ds(pl.multiple_of(which * functionals, functionals), functionals) for which in (mine, 1 - mine)
    )
    copies = (
        pltpu.make_async_copy(received, out.at[:, other], sems.at[0]),
        pltpu.make_async_copy(mine_sums, sums.at[at], sems.at[1]),
        pltpu.make_async_copy(other_sums, sums.at[other], sems.at[2]),
    )
    for copy in copies:
        copy.start()
    for copy in copies:
        copy.wait()


def assemble_kernel(own, peer, cross, diag, horiz, planes, row_near, row_far):
    layer = lax.axis_index("layer")
    count, rows = own.shape[0], own.shape[1]
    for k, block in ((0, own), (1, peer), (3, cross), (2, diag)):
        start = pl.multiple_of(jnp.bitwise_xor(layer, k) * LANES, LANES)
        planes[0:count, :, pl.ds(start, LANES)] = block[...]
    planes[count] = horiz[...]
    for k in range(row_near.shape[0]):
        at = min(k, count)
        near, far = paired_rows(planes[at, 0:1, :], planes[at, rows - 1 : rows, :])
        row_near[k : k + 1, :] = near
        row_far[k : k + 1, :] = far


def local_kernel(own, received, planes, local, boundary, factors):
    side, core = position()
    layers = planes.shape[0] - 3
    half, functionals, rows, _ = local.shape
    held = half // 2
    multiplier, inverse, _ = chip_factors(lambda k: planes[k], side, layers)
    for j in range(half):
        factors[0, j] = multiplier[j + 1]
        factors[1, j] = inverse[j]

    def sweep(at_side, at_core):
        order = range(half) if at_side == 0 else range(half - 1, -1, -1)

        def step(f, carry):
            values = [(own if m // held == at_core else received)[m % held, f] for m in order]
            solved = chip_solve(
                values,
                [None] + [factors[0, j] for j in range(half)],
                [factors[1, j] for j in range(half)],
            )
            for j in range(half):
                local[j, f] = solved[j]
            boundary[f] = solved[half - 1]
            return carry

        lax.fori_loop(0, functionals, step, 0, unroll=8)

    for at_side in range(2):
        for at_core in range(2):
            pl.when((side == at_side) & (core == at_core))(
                functools.partial(sweep, at_side, at_core)
            )


def full_factors(get, layers):
    multiplier, inverse = [None], []
    horiz = get(layers + 2)
    low = get(0)
    for k in range(layers):
        high = get(k + 1) if k + 1 < layers else jnp.zeros_like(low)
        pivot = low + high + 4.0 * horiz
        if k > 0:
            pivot = pivot - low * multiplier[k]
        inverse.append(1.0 / pivot)
        multiplier.append(high * inverse[k])
        low = high
    return multiplier, inverse


def bed_row(multiplier, inverse):
    layers = len(inverse)
    swept = [jnp.ones_like(inverse[0])]
    for k in range(1, layers):
        swept.append(multiplier[k] * swept[k - 1])
    solved = [None] * layers
    solved[layers - 1] = swept[layers - 1] * inverse[layers - 1]
    for k in range(layers - 2, -1, -1):
        solved[k] = swept[k] * inverse[k] + multiplier[k + 1] * solved[k + 1]
    return solved


def grouped(values, labels):
    label = labels.astype(jnp.int32)
    parts = []
    for b in range(GROUPS // LANES):
        inside = jnp.broadcast_to((label // LANES) == b, values.shape)
        parts.append(jnp.where(inside, values, 0.0))
    left = jnp.concatenate(parts, axis=0)
    high = left.astype(jnp.bfloat16)
    rest = left - high.astype(jnp.float32)
    middle = rest.astype(jnp.bfloat16)
    low = (rest - middle.astype(jnp.float32)).astype(jnp.bfloat16)
    left = jnp.concatenate([high, middle, low], axis=0)
    place = lax.broadcasted_iota(jnp.int32, (LANES, values.shape[1]), 0)
    match = jnp.where(jnp.broadcast_to(label % LANES, place.shape) == place, 1.0, 0.0)
    return lax.dot_general(
        left,
        match.astype(jnp.bfloat16),
        (((1,), (1,)), ((), ())),
        preferred_element_type=jnp.float32,
    )


def add_groups(sums, total, scale, functionals):
    blocks = GROUPS // LANES
    size = blocks * functionals
    total = (total[0:size] + total[size : 2 * size] + total[2 * size :]) * scale
    for b in range(blocks):
        lanes = slice(b * LANES, (b + 1) * LANES)
        sums[:, lanes] = sums[:, lanes] + total[b * functionals : (b + 1) * functionals]


def column_kernel(own, received, planes, sums, weights, parts, terms, *, scale):
    side, core = position()
    layers = planes.shape[0] - 3
    held, functionals, rows, width = own.shape
    half = 2 * held
    multiplier, inverse = full_factors(lambda k: planes[k], layers)
    weight = planes[layers]
    spread = weight * planes[layers + 2]
    for k, value in enumerate(bed_row(multiplier, inverse)):
        weights[4, k] = value
    for direction in (UP, DOWN, LEFT, RIGHT):
        source = [moved(weights[4, k] * spread, direction) for k in range(layers)]
        for k, value in enumerate(chip_solve(source, multiplier, inverse)):
            weights[direction, k] = value
    for k in range(layers):
        weights[4, k] = weights[4, k] * weight

    def chunk(n, carry):
        lanes = pl.ds(pl.multiple_of(n * LANES, LANES), LANES)
        totals = [[None] * functionals for _ in range(5)]
        for source, first in ((own, core * held), (received, (1 - core) * held)):
            for i in range(held):
                factor = [weights[kind, side * half + first + i, :, lanes] for kind in range(5)]
                for f in range(functionals):
                    value = source[i, f, :, lanes]
                    for kind in range(5):
                        term = value * factor[kind]
                        old = totals[kind][f]
                        totals[kind][f] = term if old is None else old + term
        for kind in range(5):
            for f in range(functionals):
                parts[kind, f, :, lanes] = totals[kind][f]
        return carry

    lax.fori_loop(0, width // LANES, chunk, 0, unroll=4)

    def step(f, carry):
        here = parts[4, f] + moved(parts[UP, f], DOWN) + moved(parts[DOWN, f], UP)
        terms[f] = here + moved(parts[LEFT, f], RIGHT) + moved(parts[RIGHT, f], LEFT)
        return carry

    lax.fori_loop(0, functionals, step, 0, unroll=8)
    total = grouped(terms[:, 0, :], planes[layers + 1, 0:1, :])
    for y in range(1, rows):
        total = total + grouped(terms[:, y, :], planes[layers + 1, y : y + 1, :])
    sums[...] = jnp.zeros_like(sums)
    add_groups(sums, total, scale, functionals)


def border_kernel(local, planes, near, far, inside, sums, halo, *, scale):
    side, _ = position()
    layers = planes.shape[0] - 3
    half, functionals, rows, _ = local.shape
    top_row = lax.broadcasted_iota(jnp.int32, halo.shape[1:], 0) == 0
    has_above, has_below = edge_flags()

    def pair(above, below):
        return jnp.where(
            top_row, jnp.broadcast_to(above, halo.shape[1:]), jnp.broadcast_to(below, halo.shape[1:])
        )

    for k in range(layers + 3):
        halo[k] = pair(*halo_rows(near[k : k + 1, :], far[k : k + 1, :]))
    live = halo[layers] * halo[layers + 2] * jnp.where(top_row, has_above, has_below)
    lower, lower_inverse, kappa = chip_factors(lambda k: halo[k], 0, layers)
    upper, upper_inverse, _ = chip_factors(lambda k: halo[k], 1, layers)
    lower_unit, upper_unit = unit_response(lower, lower_inverse), unit_response(upper, upper_inverse)
    bed = chip_solve(
        [jnp.ones_like(kappa)] + [jnp.zeros_like(kappa)] * (half - 1), lower, lower_inverse
    )
    below_top = kappa * bed[half - 1] / (1.0 - kappa * lower_unit[half - 1] * kappa * upper_unit[half - 1])
    above_top = kappa * upper_unit[half - 1] * below_top
    lower_row = [live * (bed[j] + lower_unit[j] * above_top) for j in range(half)]
    upper_row = [live * (upper_unit[j] * below_top) for j in range(half)]
    mine = [jnp.where(side == 0, a, b) for a, b in zip(lower_row, upper_row)]
    other = [jnp.where(side == 0, b, a) for a, b in zip(lower_row, upper_row)]

    def edge(k):
        return pair(planes[k, 0:1, :], planes[k, rows - 1 : rows, :])

    multiplier, inverse, kappa = chip_factors(edge, side, layers)
    unit = unit_response(multiplier, inverse)
    unit_other = unit_response(*chip_factors(edge, 1 - side, layers)[:2])
    reach, reach_other = unit[0] * mine[0], unit_other[0] * other[0]
    for j in range(1, half):
        reach = reach + unit[j] * mine[j]
        reach_other = reach_other + unit_other[j] * other[j]
    far_side = kappa * unit_other[half - 1]
    across = (reach_other + far_side * reach) / (1.0 - kappa * unit[half - 1] * far_side)
    mine[half - 1] = mine[half - 1] + kappa * across
    sums[...] = inside[...]
    total = None
    for which, row in enumerate((0, rows - 1)):
        out = local[0, :, row, :] * mine[0][which : which + 1]
        for j in range(1, half):
            out = out + local[j, :, row, :] * mine[j][which : which + 1]
        part = grouped(out, halo[layers + 1, which : which + 1, :])
        total = part if total is None else total + part
    add_groups(sums, total, scale, functionals)


def fold_kernel(mine, *refs):
    parts, message, out = refs[:-2], refs[-2], refs[-1]
    total = mine[...]
    if parts:
        total = total + parts[0][...]
    if len(parts) == 3:
        total = total + (parts[1][...] + parts[2][...])
    size = mine.shape[0]
    out[out.shape[0] - size :, :] = total


def middle_kernel(local, planes, halo, near, far, base, message, factors, outside):
    side, _ = position()
    layers = planes.shape[0] - 3
    half, functionals, rows, _ = local.shape
    multiplier, inverse, _ = chip_factors(lambda k: halo[k], side, layers)
    around = []
    for m in range(half):
        at = slice(m * functionals, (m + 1) * functionals)
        around.append(halo_rows(near[at, :], far[at, :]))
    for which, live in enumerate(edge_flags()):
        values = [
            jnp.where(side == 0, around[j][which], around[half - 1 - j][which]) for j in range(half)
        ]
        solved = chip_solve(
            values,
            [None] + [m[which : which + 1] for m in multiplier[1:]],
            [v[which : which + 1] for v in inverse],
        )
        for j in range(half):
            outside[which, j] = solved[j] * live
        start = functionals * (rows + which)
        message[start : start + functionals, :] = solved[half - 1]
    multiplier, inverse, _ = chip_factors(lambda k: planes[k], side, layers)
    for j in range(half):
        factors[0, j] = multiplier[j + 1]
        factors[1, j] = inverse[j]

    def step(f, carry):
        horiz = planes[layers + 2]
        residual = []
        for j in range(half):
            here = local[j, f]
            at = pl.ds(f, 1)
            around = moved(here, UP, outside[0, j, at, :]) + moved(here, DOWN, outside[1, j, at, :])
            around = around + moved(here, LEFT) + moved(here, RIGHT)
            residual.append(horiz * around)
        solved = chip_solve(
            residual,
            [None] + [factors[0, j] for j in range(half)],
            [factors[1, j] for j in range(half)],
        )
        for j in range(half):
            solved[j] = local[j, f] + solved[j]
            base[j, f] = solved[j]
        message[pl.ds(pl.multiple_of(f * rows, rows), rows), :] = solved[half - 1]
        return carry

    lax.fori_loop(0, functionals, step, 0, unroll=8)


def coefficient_kernel(planes, halo, spread, spread_other, response, ends, halo_response):
    side, _ = position()
    layers = planes.shape[0] - 3
    half = layers // 2
    has_above, has_below = edge_flags()
    top_row = lax.broadcasted_iota(jnp.int32, halo.shape[1:], 0) == 0
    halo_live = jnp.where(top_row, has_above, has_below)

    def both(get):
        multiplier, inverse, kappa = chip_factors(get, side, layers)
        unit = unit_response(multiplier, inverse)
        multiplier_other, inverse_other, _ = chip_factors(get, 1 - side, layers)
        unit_other = unit_response(multiplier_other, inverse_other)
        mine, other = kappa * unit[half - 1], kappa * unit_other[half - 1]
        return multiplier, inverse, kappa, unit, unit_other, (mine, other, 1.0 / (1.0 - mine * other))

    _, _, kappa, unit, unit_other, corner = both(lambda k: halo[k])
    rows_halo = halo.shape[1]
    for i in range(3):
        ends[i + 3, 0:rows_halo] = corner[i] * halo_live if i == 2 else corner[i]
    for j in range(half):
        halo_response[0, j] = kappa * unit[j] * halo_live
        halo_response[1, j] = kappa * unit_other[j] * halo_live
    multiplier, inverse, kappa, unit, unit_other, corner = both(lambda k: planes[k])
    for i in range(3):
        ends[i] = corner[i]
    horiz = planes[layers + 2]
    mine = [kappa * unit[j] for j in range(half)]
    other = [kappa * unit_other[j] for j in range(half)]
    for j in range(half):
        response[j] = mine[j]
    for direction in (UP, DOWN, LEFT, RIGHT):
        source, total = [], jnp.zeros_like(horiz)
        for j in range(half):
            edges = (None, None)
            if direction in (UP, DOWN):
                edges = tuple(halo_response[i, j, direction : direction + 1, :] for i in range(2))
            source.append(horiz * moved(mine[j], direction, edges[0]))
            total = total + unit_other[j] * moved(other[j], direction, edges[1])
        spread_other[direction] = horiz * total
        for j, value in enumerate(chip_solve(source, multiplier, inverse)):
            spread[direction, j] = value


def interface_kernel(
    base, boundary, boundary_other, message_mine, message, spread, spread_other, ends, near, diag,
    around_all, second_all, sums, halo_mine, halo_other,
):
    half, functionals, rows, _ = base.shape
    last = functionals * (rows + 2)
    sums[...] = message_mine[last:, :] + message[last:, :]
    if near is not None:
        sums[...] = sums[...] + (near[...] + diag[...])
    for i in range(2):
        start = functionals * (rows + i)
        here = message_mine[start : start + functionals, :]
        mine, other, inverse = (ends[k, i : i + 1, :] for k in (3, 4, 5))
        live = jnp.where(inverse == 0.0, 0.0, 1.0)
        value = (message[start : start + functionals, :] + other * here) * inverse
        halo_other[i] = value
        halo_mine[i] = (here + mine * value) * live

    def step(f, carry):
        here = boundary[f]
        mine, other, inverse = ends[0], ends[1], ends[2]
        value = (boundary_other[f] + other * here) * inverse
        value_mine = here + mine * value

        def around(plane, edges):
            return [
                moved(plane, UP, edges[0, pl.ds(f, 1), :]),
                moved(plane, DOWN, edges[1, pl.ds(f, 1), :]),
                moved(plane, LEFT),
                moved(plane, RIGHT),
            ]

        value_around = around(value, halo_other)
        mine_around = around(value_mine, halo_mine)
        last = base[half - 1, f]
        last_other = message[pl.ds(pl.multiple_of(f * rows, rows), rows), :]
        for d in range(4):
            around_all[d, f] = value_around[d]
            last = last + spread[d, half - 1] * value_around[d]
            last_other = last_other + spread_other[d] * mine_around[d]
        second_all[f] = (last_other + other * last) * inverse
        return carry

    lax.fori_loop(0, functionals, step, 0, unroll=8)


def final_kernel(base, around_all, second_all, spread, response, out, *, other_core):
    side, core = position()
    half, functionals = base.shape[0], base.shape[1]
    held = half // 2
    group = 1 - core if other_core else core

    def step(f, carry):
        second = second_all[f]
        value_around = [around_all[d, f] for d in range(4)]
        for i in range(held):
            m = group * held + i
            j = jnp.where(side == 0, m, half - 1 - m)
            value = base[j, f] + response[j] * second
            for d in range(4):
                value = value + spread[d, j] * value_around[d]
            out[i, f] = value
        return carry

    lax.fori_loop(0, functionals, step, 0, unroll=8)


def call(
    kernel, out_shapes, scratch=(), any_inputs=(), hbm_inputs=(), any_outputs=(), aliases=None
):
    def run(*operands):
        spaces = [
            pltpu.HBM if i in hbm_inputs else pl.ANY if i in any_inputs else pltpu.VMEM
            for i in range(len(operands))
        ]
        in_specs = [pl.BlockSpec(memory_space=space) for space in spaces]
        operands = [
            pltpu.with_memory_space_constraint(x, pltpu.HBM) if space is pltpu.HBM else x
            for x, space in zip(operands, spaces)
        ]
        return pl.pallas_call(
            kernel,
            out_shape=[
                (pltpu.HBM if i in any_outputs else jax.ShapeDtypeStruct)(s, jnp.float32)
                for i, s in enumerate(out_shapes)
            ],
            in_specs=in_specs,
            out_specs=[
                pl.BlockSpec(memory_space=pltpu.HBM if i in any_outputs else pltpu.VMEM)
                for i in range(len(out_shapes))
            ],
            scratch_shapes=list(scratch),
            input_output_aliases=aliases or {},
            compiler_params=pltpu.CompilerParams(vmem_limit_bytes=VMEM_BYTES),
        )(*operands)

    return run


def add_parts(values, parts):
    values = values + parts[0]
    return values + (parts[1] + parts[2]) if len(parts) == 3 else values


def after(value, *earlier):
    return lax.optimization_barrier((value, *earlier))[0]


def shards(forcing, vert_coupling, horiz_coupling, basal_velocity, group_label, ice_mask):
    layers, rows, width_block = vert_coupling.shape
    held, functionals_all, _, width = forcing.shape
    half, functionals = layers // 2, functionals_all // 2
    tiles = lax.axis_size("tile")
    f32 = jnp.float32

    def send(array, target):
        pairs = []
        for t in range(tiles):
            for i in range(4):
                u, k = target(t, i)
                pairs.append((4 * t + i, 4 * u + k))
        return lax.ppermute(array, ("tile", "layer"), pairs)

    def across(array, bits):
        return send(array, lambda t, i: (t, i ^ bits))

    def parity(t):
        return bin(t).count("1") % 2

    def to_near(array, bits=None):
        return to_tile(array, bits, lambda t: t ^ 1)

    def to_far(array, bits=None):
        return to_tile(array, bits, lambda t: t + 1 if t % 2 else t - 1)

    def to_tile(array, bits, partner):
        def target(t, i):
            u = partner(t)
            if not 0 <= u < tiles:
                return t, i ^ 1
            return u, i ^ ((parity(t) + parity(u)) % 2 if bits is None else bits)

        return send(array, target)

    def exchange(values, masks):
        kinds = list(masks)
        if len(masks) == 2:
            kinds.append(masks[0] | masks[1])
        return [send(values, lambda t, i: (t ^ d, i ^ (n < 2))) for n, d in enumerate(kinds)]

    dma = pltpu.SemaphoreType.DMA
    count = layers + 3
    edge_rows = -(-count // 8) * 8
    stack = half * functionals
    flat = (rows, width_block)
    quarter = (held, functionals, rows, width)
    join = lax.optimization_barrier
    block, forcing_sent, forcing_kept = call(
        pack_kernel,
        [(layers + 2, *flat), quarter, quarter],
        [pltpu.VMEM(flat, f32), pltpu.VMEM(flat, jnp.int32), pltpu.VMEM(flat, jnp.int32), dma((6,))],
        hbm_inputs=range(5),
    )(vert_coupling, basal_velocity, group_label, ice_mask, forcing)
    cross, peer, forcing_received = join(
        (across(block, 3), across(block, 1), across(forcing_sent, 1))
    )
    rows_near, rows_far = call(rows_kernel, [(stack, width), (stack, width)])(
        forcing_kept, forcing_received
    )
    rows_far = to_far(rows_far)
    rows_near = to_near(rows_near)
    diag = across(cross, 1)
    planes, edge_near, edge_far = call(
        assemble_kernel, [(count, rows, width), (edge_rows, width), (edge_rows, width)]
    )(block, peer, cross, diag, horiz_coupling)
    edge_far = to_far(edge_far, 1)
    edge_near = to_near(edge_near, 1)

    factors = pltpu.VMEM((2, half, rows, width), f32)
    columns_all = tiles * rows * width
    scale = -((columns_all / GROUPS) ** -0.5)
    (sums_inside,) = call(
        functools.partial(column_kernel, scale=scale),
        [(functionals, GROUPS)],
        [
            pltpu.VMEM((5, layers, rows, width), f32),
            pltpu.VMEM((5, functionals, rows, width), f32),
            pltpu.VMEM((functionals, rows, width), f32),
        ],
    )(forcing_kept, forcing_received, planes)
    planes_later, edge_near, edge_far, sums_inside = join((planes, edge_near, edge_far, sums_inside))
    local, boundary = call(
        local_kernel,
        [(half, functionals, rows, width), (functionals, rows, width)],
        [factors],
    )(forcing_kept, forcing_received, planes)
    sums, halo = call(
        functools.partial(border_kernel, scale=scale),
        [(functionals, GROUPS), (count, 8, width)],
    )(local, planes, edge_near, edge_far, sums_inside)

    boundary_other = across(after(boundary, sums_inside), 3)
    spread, spread_other, response, ends = call(
        coefficient_kernel,
        [(4, half, rows, width), (4, rows, width), (half, rows, width), (6, rows, width)],
        [pltpu.VMEM((2, half, 8, width), f32)],
    )(planes, halo)

    masks = [1 << bit for bit in range(1, (tiles - 1).bit_length())]
    while len(masks) > 2:
        sums = add_parts(sums, exchange(sums, masks[:2]))
        masks = masks[2:]
    parts = exchange(sums, masks)
    base, message = call(
        middle_kernel,
        [(half, functionals, rows, width), (functionals * (rows + 3), width)],
        [factors, pltpu.VMEM((2, half, functionals, width), f32)],
    )(after(local, spread), planes, halo, rows_near, rows_far)
    (message,) = call(
        fold_kernel,
        [message.shape],
        aliases={len(parts) + 1: 0},
    )(after(sums, boundary_other), *parts, message)
    message_other = across(message, 3)
    sums = message[functionals * (rows + 2) :]
    near = send(sums, lambda t, i: (t ^ 1, i ^ 1))
    diag = send(sums, lambda t, i: (t ^ 1, i ^ 2))
    message_other, near, diag = join((message_other, near, diag))
    halo_rows_both = pltpu.VMEM((2, functionals, width), f32)
    around, second, sums = call(
        interface_kernel,
        [(4, functionals, rows, width), (functionals, rows, width), (functionals, GROUPS)],
        [halo_rows_both, halo_rows_both],
    )(base, boundary, boundary_other, message, message_other, spread, spread_other, ends, near, diag)
    (sent,) = call(functools.partial(final_kernel, other_core=True), [quarter])(
        base, around, second, spread, response
    )
    (kept,) = call(functools.partial(final_kernel, other_core=False), [quarter])(
        base, around, second, spread, response
    )
    whole = (held, functionals_all, rows, width)
    (partly,) = call(place_kept_kernel, [whole], [dma], any_inputs=(0,), any_outputs=(0,))(kept)
    received, other_sums, partly = join((across(sent, 1), across(sums, 1), partly))
    adjoint, sums = call(
        place_kernel,
        [whole, (functionals_all, GROUPS)],
        [dma((3,))],
        any_inputs=(1, 2, 3),
        hbm_inputs=(0,),
        any_outputs=(0, 1),
        aliases={0: 0},
    )(partly, received, sums, other_sums)
    return (adjoint, sums)


def solution(mesh):
    in_specs = (
        P("layer", None, "tile", None),
        P(None, "tile", "layer"),
        P("tile", None),
        P("tile", "layer"),
        P("tile", "layer"),
        P("tile", "layer"),
    )
    out_specs = (P("layer", None, "tile", None), P())
    return jax.shard_map(shards, mesh=mesh, in_specs=in_specs, out_specs=out_specs, check_vma=False)
```

```python
import functools

import jax
import jax.numpy as jnp
from jax import lax
from jax.experimental import pallas as pl
from jax.experimental.pallas import tpu as pltpu
from jax.sharding import PartitionSpec as P

GROUPS = 512
LANES = 128
VMEM_BYTES = 32 * 1024 * 1024
UP, DOWN, LEFT, RIGHT = range(4)


def position():
    layer = lax.axis_index("layer")
    return layer // 2, layer % 2


def owned_half():
    side, core = position()
    tile = lax.axis_index("tile")
    total = side + core
    for bit in range((lax.axis_size("tile") - 1).bit_length()):
        total = total + lax.shift_right_logical(tile, bit) % 2
    return total % 2


def edge_flags():
    tile = lax.axis_index("tile")
    last = lax.axis_size("tile") - 1
    return (
        jnp.where(tile > 0, 1.0, 0.0).astype(jnp.float32),
        jnp.where(tile < last, 1.0, 0.0).astype(jnp.float32),
    )


def paired_rows(first, last):
    even = lax.axis_index("tile") % 2 == 0
    return jnp.where(even, last, first), jnp.where(even, first, last)


def halo_rows(near, far):
    even = lax.axis_index("tile") % 2 == 0
    return jnp.where(even, far, near), jnp.where(even, near, far)


def moved(plane, direction, halo=None):
    rows, width = plane.shape
    axis = 0 if direction in (UP, DOWN) else 1
    size = plane.shape[axis]
    first = direction in (UP, LEFT)
    rolled = pltpu.roll(plane, 1 if first else size - 1, axis)
    at_edge = lax.broadcasted_iota(jnp.int32, plane.shape, axis) == (0 if first else size - 1)
    filler = jnp.zeros_like(plane) if halo is None else jnp.broadcast_to(halo, plane.shape)
    return jnp.where(at_edge, filler, rolled)


def chip_factors(planes, side, layers):
    half = layers // 2
    horiz = planes(layers + 2)

    def coupling(j):
        if j == 0:
            return planes(0) * jnp.where(side == 0, 1.0, 0.0)
        return planes(jnp.where(side == 0, j, layers - j))

    multiplier, inverse = [None], []
    below = coupling(0)
    for j in range(half):
        above = coupling(j + 1)
        pivot = below + above + 4.0 * horiz
        if j > 0:
            pivot = pivot - below * multiplier[j]
        inverse.append(1.0 / pivot)
        multiplier.append(above * inverse[j])
        below = above
    return multiplier, inverse, below


def unit_response(multiplier, inverse):
    half = len(inverse)
    response = [None] * half
    response[half - 1] = inverse[half - 1]
    for j in range(half - 2, -1, -1):
        response[j] = multiplier[j + 1] * response[j + 1]
    return response


def chip_solve(values, multiplier, inverse):
    half = len(values)
    swept = [values[0]]
    for j in range(1, half):
        swept.append(values[j] + multiplier[j] * swept[j - 1])
    solved = [None] * half
    solved[half - 1] = swept[half - 1] * inverse[half - 1]
    for j in range(half - 2, -1, -1):
        solved[j] = swept[j] * inverse[j] + multiplier[j + 1] * solved[j + 1]
    return solved


def pack_kernel(
    coupling, velocity, label, mask, forcing, block, sent, kept, velocity_in, label_in, mask_in, sems
):
    mine = owned_half()
    layers = coupling.shape[0]
    functionals = sent.shape[1]
    pairs = [
        (coupling, block.at[pl.ds(0, layers)]),
        (velocity, velocity_in),
        (label, label_in),
        (mask, mask_in),
    ]
    for target, which in ((sent, 1 - mine), (kept, mine)):
        pairs.append((forcing.at[:, pl.ds(which * functionals, functionals)], target))
    copies = [pltpu.make_async_copy(a, b, sems.at[i]) for i, (a, b) in enumerate(pairs)]
    for copy in copies:
        copy.start()
    for copy in copies[:4]:
        copy.wait()
    block[layers] = block[0] * velocity_in[...] * mask_in[...].astype(jnp.float32)
    block[layers + 1] = label_in[...].astype(jnp.float32)
    for copy in copies[4:]:
        copy.wait()


def rows_kernel(kept, received, row_near, row_far):
    _, core = position()
    held, functionals, rows, _ = kept.shape
    for source, first in ((kept, core * held), (received, (1 - core) * held)):
        for i in range(held):
            near, far = paired_rows(source[i, :, 0, :], source[i, :, rows - 1, :])
            at = pl.ds(pl.multiple_of((first + i) * functionals, functionals), functionals)
            row_near[at, :] = near
            row_far[at, :] = far


def place_kept_kernel(kept, out, sem):
    functionals = kept.shape[1]
    at = pl.ds(pl.multiple_of(owned_half() * functionals, functionals), functionals)
    copy = pltpu.make_async_copy(kept, out.at[:, at], sem)
    copy.start()
    copy.wait()


def place_kernel(partly, received, mine_sums, other_sums, out, sums, sems):
    mine = owned_half()
    functionals = received.shape[1]
    at, other = (
        pl.ds(pl.multiple_of(which * functionals, functionals), functionals) for which in (mine, 1 - mine)
    )
    copies = (
        pltpu.make_async_copy(received, out.at[:, other], sems.at[0]),
        pltpu.make_async_copy(mine_sums, sums.at[at], sems.at[1]),
        pltpu.make_async_copy(other_sums, sums.at[other], sems.at[2]),
    )
    for copy in copies:
        copy.start()
    for copy in copies:
        copy.wait()


def assemble_kernel(own, peer, cross, diag, horiz, planes, row_near, row_far):
    layer = lax.axis_index("layer")
    count, rows = own.shape[0], own.shape[1]
    for k, block in ((0, own), (1, peer), (3, cross), (2, diag)):
        start = pl.multiple_of(jnp.bitwise_xor(layer, k) * LANES, LANES)
        planes[0:count, :, pl.ds(start, LANES)] = block[...]
    planes[count] = horiz[...]
    for k in range(row_near.shape[0]):
        at = min(k, count)
        near, far = paired_rows(planes[at, 0:1, :], planes[at, rows - 1 : rows, :])
        row_near[k : k + 1, :] = near
        row_far[k : k + 1, :] = far


def local_kernel(own, received, planes, local, boundary, factors):
    side, core = position()
    layers = planes.shape[0] - 3
    half, functionals, rows, _ = local.shape
    held = half // 2
    multiplier, inverse, _ = chip_factors(lambda k: planes[k], side, layers)
    for j in range(half):
        factors[0, j] = multiplier[j + 1]
        factors[1, j] = inverse[j]

    def sweep(at_side, at_core):
        order = range(half) if at_side == 0 else range(half - 1, -1, -1)

        def step(f, carry):
            values = [(own if m // held == at_core else received)[m % held, f] for m in order]
            solved = chip_solve(
                values,
                [None] + [factors[0, j] for j in range(half)],
                [factors[1, j] for j in range(half)],
            )
            for j in range(half):
                local[j, f] = solved[j]
            boundary[f] = solved[half - 1]
            return carry

        lax.fori_loop(0, functionals, step, 0, unroll=8)

    for at_side in range(2):
        for at_core in range(2):
            pl.when((side == at_side) & (core == at_core))(
                functools.partial(sweep, at_side, at_core)
            )


def full_factors(get, layers):
    multiplier, inverse = [None], []
    horiz = get(layers + 2)
    low = get(0)
    for k in range(layers):
        high = get(k + 1) if k + 1 < layers else jnp.zeros_like(low)
        pivot = low + high + 4.0 * horiz
        if k > 0:
            pivot = pivot - low * multiplier[k]
        inverse.append(1.0 / pivot)
        multiplier.append(high * inverse[k])
        low = high
    return multiplier, inverse


def bed_row(multiplier, inverse):
    layers = len(inverse)
    swept = [jnp.ones_like(inverse[0])]
    for k in range(1, layers):
        swept.append(multiplier[k] * swept[k - 1])
    solved = [None] * layers
    solved[layers - 1] = swept[layers - 1] * inverse[layers - 1]
    for k in range(layers - 2, -1, -1):
        solved[k] = swept[k] * inverse[k] + multiplier[k + 1] * solved[k + 1]
    return solved


def grouped(values, labels):
    label = labels.astype(jnp.int32)
    parts = []
    for b in range(GROUPS // LANES):
        inside = jnp.broadcast_to((label // LANES) == b, values.shape)
        parts.append(jnp.where(inside, values, 0.0))
    left = jnp.concatenate(parts, axis=0)
    high = left.astype(jnp.bfloat16)
    rest = left - high.astype(jnp.float32)
    middle = rest.astype(jnp.bfloat16)
    low = (rest - middle.astype(jnp.float32)).astype(jnp.bfloat16)
    left = jnp.concatenate([high, middle, low], axis=0)
    place = lax.broadcasted_iota(jnp.int32, (LANES, values.shape[1]), 0)
    match = jnp.where(jnp.broadcast_to(label % LANES, place.shape) == place, 1.0, 0.0)
    return lax.dot_general(
        left,
        match.astype(jnp.bfloat16),
        (((1,), (1,)), ((), ())),
        preferred_element_type=jnp.float32,
    )


def add_groups(sums, total, scale, functionals):
    blocks = GROUPS // LANES
    size = blocks * functionals
    total = (total[0:size] + total[size : 2 * size] + total[2 * size :]) * scale
    for b in range(blocks):
        lanes = slice(b * LANES, (b + 1) * LANES)
        sums[:, lanes] = sums[:, lanes] + total[b * functionals : (b + 1) * functionals]


def column_kernel(own, received, planes, sums, weights, parts, terms, *, scale):
    side, core = position()
    layers = planes.shape[0] - 3
    held, functionals, rows, width = own.shape
    half = 2 * held
    multiplier, inverse = full_factors(lambda k: planes[k], layers)
    weight = planes[layers]
    spread = weight * planes[layers + 2]
    for k, value in enumerate(bed_row(multiplier, inverse)):
        weights[4, k] = value
    for direction in (UP, DOWN, LEFT, RIGHT):
        source = [moved(weights[4, k] * spread, direction) for k in range(layers)]
        for k, value in enumerate(chip_solve(source, multiplier, inverse)):
            weights[direction, k] = value
    for k in range(layers):
        weights[4, k] = weights[4, k] * weight

    def chunk(n, carry):
        lanes = pl.ds(pl.multiple_of(n * LANES, LANES), LANES)
        totals = [[None] * functionals for _ in range(5)]
        for source, first in ((own, core * held), (received, (1 - core) * held)):
            for i in range(held):
                factor = [weights[kind, side * half + first + i, :, lanes] for kind in range(5)]
                for f in range(functionals):
                    value = source[i, f, :, lanes]
                    for kind in range(5):
                        term = value * factor[kind]
                        old = totals[kind][f]
                        totals[kind][f] = term if old is None else old + term
        for kind in range(5):
            for f in range(functionals):
                parts[kind, f, :, lanes] = totals[kind][f]
        return carry

    lax.fori_loop(0, width // LANES, chunk, 0, unroll=4)

    def step(f, carry):
        here = parts[4, f] + moved(parts[UP, f], DOWN) + moved(parts[DOWN, f], UP)
        terms[f] = here + moved(parts[LEFT, f], RIGHT) + moved(parts[RIGHT, f], LEFT)
        return carry

    lax.fori_loop(0, functionals, step, 0, unroll=8)
    total = grouped(terms[:, 0, :], planes[layers + 1, 0:1, :])
    for y in range(1, rows):
        total = total + grouped(terms[:, y, :], planes[layers + 1, y : y + 1, :])
    sums[...] = jnp.zeros_like(sums)
    add_groups(sums, total, scale, functionals)


def border_kernel(local, planes, near, far, inside, sums, halo, *, scale):
    side, _ = position()
    layers = planes.shape[0] - 3
    half, functionals, rows, _ = local.shape
    top_row = lax.broadcasted_iota(jnp.int32, halo.shape[1:], 0) == 0
    has_above, has_below = edge_flags()

    def pair(above, below):
        return jnp.where(
            top_row, jnp.broadcast_to(above, halo.shape[1:]), jnp.broadcast_to(below, halo.shape[1:])
        )

    for k in range(layers + 3):
        halo[k] = pair(*halo_rows(near[k : k + 1, :], far[k : k + 1, :]))
    live = halo[layers] * halo[layers + 2] * jnp.where(top_row, has_above, has_below)
    lower, lower_inverse, kappa = chip_factors(lambda k: halo[k], 0, layers)
    upper, upper_inverse, _ = chip_factors(lambda k: halo[k], 1, layers)
    lower_unit, upper_unit = unit_response(lower, lower_inverse), unit_response(upper, upper_inverse)
    bed = chip_solve(
        [jnp.ones_like(kappa)] + [jnp.zeros_like(kappa)] * (half - 1), lower, lower_inverse
    )
    below_top = kappa * bed[half - 1] / (1.0 - kappa * lower_unit[half - 1] * kappa * upper_unit[half - 1])
    above_top = kappa * upper_unit[half - 1] * below_top
    lower_row = [live * (bed[j] + lower_unit[j] * above_top) for j in range(half)]
    upper_row = [live * (upper_unit[j] * below_top) for j in range(half)]
    mine = [jnp.where(side == 0, a, b) for a, b in zip(lower_row, upper_row)]
    other = [jnp.where(side == 0, b, a) for a, b in zip(lower_row, upper_row)]

    def edge(k):
        return pair(planes[k, 0:1, :], planes[k, rows - 1 : rows, :])

    multiplier, inverse, kappa = chip_factors(edge, side, layers)
    unit = unit_response(multiplier, inverse)
    unit_other = unit_response(*chip_factors(edge, 1 - side, layers)[:2])
    reach, reach_other = unit[0] * mine[0], unit_other[0] * other[0]
    for j in range(1, half):
        reach = reach + unit[j] * mine[j]
        reach_other = reach_other + unit_other[j] * other[j]
    far_side = kappa * unit_other[half - 1]
    across = (reach_other + far_side * reach) / (1.0 - kappa * unit[half - 1] * far_side)
    mine[half - 1] = mine[half - 1] + kappa * across
    sums[...] = inside[...]
    total = None
    for which, row in enumerate((0, rows - 1)):
        out = local[0, :, row, :] * mine[0][which : which + 1]
        for j in range(1, half):
            out = out + local[j, :, row, :] * mine[j][which : which + 1]
        part = grouped(out, halo[layers + 1, which : which + 1, :])
        total = part if total is None else total + part
    add_groups(sums, total, scale, functionals)


def fold_kernel(mine, *refs):
    parts, message, out = refs[:-2], refs[-2], refs[-1]
    total = mine[...]
    if parts:
        total = total + parts[0][...]
    if len(parts) == 3:
        total = total + (parts[1][...] + parts[2][...])
    size = out.shape[0] - mine.shape[0]
    out[0:size, :] = message[0:size, :]
    out[size:, :] = total


def middle_kernel(local, planes, halo, near, far, base, message, factors, outside):
    side, _ = position()
    layers = planes.shape[0] - 3
    half, functionals, rows, _ = local.shape
    multiplier, inverse, _ = chip_factors(lambda k: halo[k], side, layers)
    around = []
    for m in range(half):
        at = slice(m * functionals, (m + 1) * functionals)
        around.append(halo_rows(near[at, :], far[at, :]))
    for which, live in enumerate(edge_flags()):
        values = [
            jnp.where(side == 0, around[j][which], around[half - 1 - j][which]) for j in range(half)
        ]
        solved = chip_solve(
            values,
            [None] + [m[which : which + 1] for m in multiplier[1:]],
            [v[which : which + 1] for v in inverse],
        )
        for j in range(half):
            outside[which, j] = solved[j] * live
        start = functionals * (rows + which)
        message[start : start + functionals, :] = solved[half - 1]
    multiplier, inverse, _ = chip_factors(lambda k: planes[k], side, layers)
    for j in range(half):
        factors[0, j] = multiplier[j + 1]
        factors[1, j] = inverse[j]

    def step(f, carry):
        horiz = planes[layers + 2]
        residual = []
        for j in range(half):
            here = local[j, f]
            at = pl.ds(f, 1)
            around = moved(here, UP, outside[0, j, at, :]) + moved(here, DOWN, outside[1, j, at, :])
            around = around + moved(here, LEFT) + moved(here, RIGHT)
            residual.append(horiz * around)
        solved = chip_solve(
            residual,
            [None] + [factors[0, j] for j in range(half)],
            [factors[1, j] for j in range(half)],
        )
        for j in range(half):
            solved[j] = local[j, f] + solved[j]
            base[j, f] = solved[j]
        message[pl.ds(pl.multiple_of(f * rows, rows), rows), :] = solved[half - 1]
        return carry

    lax.fori_loop(0, functionals, step, 0, unroll=8)


def coefficient_kernel(planes, halo, spread, spread_other, response, ends, halo_response):
    side, _ = position()
    layers = planes.shape[0] - 3
    half = layers // 2
    has_above, has_below = edge_flags()
    top_row = lax.broadcasted_iota(jnp.int32, halo.shape[1:], 0) == 0
    halo_live = jnp.where(top_row, has_above, has_below)

    def both(get):
        multiplier, inverse, kappa = chip_factors(get, side, layers)
        unit = unit_response(multiplier, inverse)
        multiplier_other, inverse_other, _ = chip_factors(get, 1 - side, layers)
        unit_other = unit_response(multiplier_other, inverse_other)
        mine, other = kappa * unit[half - 1], kappa * unit_other[half - 1]
        return multiplier, inverse, kappa, unit, unit_other, (mine, other, 1.0 / (1.0 - mine * other))

    _, _, kappa, unit, unit_other, corner = both(lambda k: halo[k])
    rows_halo = halo.shape[1]
    for i in range(3):
        ends[i + 3, 0:rows_halo] = corner[i] * halo_live if i == 2 else corner[i]
    for j in range(half):
        halo_response[0, j] = kappa * unit[j] * halo_live
        halo_response[1, j] = kappa * unit_other[j] * halo_live
    multiplier, inverse, kappa, unit, unit_other, corner = both(lambda k: planes[k])
    for i in range(3):
        ends[i] = corner[i]
    horiz = planes[layers + 2]
    mine = [kappa * unit[j] for j in range(half)]
    other = [kappa * unit_other[j] for j in range(half)]
    for j in range(half):
        response[j] = mine[j]
    for direction in (UP, DOWN, LEFT, RIGHT):
        source, total = [], jnp.zeros_like(horiz)
        for j in range(half):
            edges = (None, None)
            if direction in (UP, DOWN):
                edges = tuple(halo_response[i, j, direction : direction + 1, :] for i in range(2))
            source.append(horiz * moved(mine[j], direction, edges[0]))
            total = total + unit_other[j] * moved(other[j], direction, edges[1])
        spread_other[direction] = horiz * total
        for j, value in enumerate(chip_solve(source, multiplier, inverse)):
            spread[direction, j] = value


def interface_kernel(
    base, boundary, boundary_other, message_mine, message, spread, spread_other, ends, near, diag,
    around_all, second_all, sums, halo_mine, halo_other,
):
    half, functionals, rows, _ = base.shape
    last = functionals * (rows + 2)
    sums[...] = message_mine[last:, :] + message[last:, :]
    if near is not None:
        sums[...] = sums[...] + (near[...] + diag[...])
    for i in range(2):
        start = functionals * (rows + i)
        here = message_mine[start : start + functionals, :]
        mine, other, inverse = (ends[k, i : i + 1, :] for k in (3, 4, 5))
        live = jnp.where(inverse == 0.0, 0.0, 1.0)
        value = (message[start : start + functionals, :] + other * here) * inverse
        halo_other[i] = value
        halo_mine[i] = (here + mine * value) * live

    def step(f, carry):
        here = boundary[f]
        mine, other, inverse = ends[0], ends[1], ends[2]
        value = (boundary_other[f] + other * here) * inverse
        value_mine = here + mine * value

        def around(plane, edges):
            return [
                moved(plane, UP, edges[0, pl.ds(f, 1), :]),
                moved(plane, DOWN, edges[1, pl.ds(f, 1), :]),
                moved(plane, LEFT),
                moved(plane, RIGHT),
            ]

        value_around = around(value, halo_other)
        mine_around = around(value_mine, halo_mine)
        last = base[half - 1, f]
        last_other = message[pl.ds(pl.multiple_of(f * rows, rows), rows), :]
        for d in range(4):
            around_all[d, f] = value_around[d]
            last = last + spread[d, half - 1] * value_around[d]
            last_other = last_other + spread_other[d] * mine_around[d]
        second_all[f] = (last_other + other * last) * inverse
        return carry

    lax.fori_loop(0, functionals, step, 0, unroll=8)


def final_kernel(base, around_all, second_all, spread, response, out, *, other_core):
    side, core = position()
    half, functionals = base.shape[0], base.shape[1]
    held = half // 2
    group = 1 - core if other_core else core

    def step(f, carry):
        second = second_all[f]
        value_around = [around_all[d, f] for d in range(4)]
        for i in range(held):
            m = group * held + i
            j = jnp.where(side == 0, m, half - 1 - m)
            value = base[j, f] + response[j] * second
            for d in range(4):
                value = value + spread[d, j] * value_around[d]
            out[i, f] = value
        return carry

    lax.fori_loop(0, functionals, step, 0, unroll=8)


def call(
    kernel, out_shapes, scratch=(), any_inputs=(), hbm_inputs=(), any_outputs=(), aliases=None
):
    def run(*operands):
        spaces = [
            pltpu.HBM if i in hbm_inputs else pl.ANY if i in any_inputs else pltpu.VMEM
            for i in range(len(operands))
        ]
        in_specs = [pl.BlockSpec(memory_space=space) for space in spaces]
        operands = [
            pltpu.with_memory_space_constraint(x, pltpu.HBM) if space is pltpu.HBM else x
            for x, space in zip(operands, spaces)
        ]
        return pl.pallas_call(
            kernel,
            out_shape=[
                (pltpu.HBM if i in any_outputs else jax.ShapeDtypeStruct)(s, jnp.float32)
                for i, s in enumerate(out_shapes)
            ],
            in_specs=in_specs,
            out_specs=[
                pl.BlockSpec(memory_space=pltpu.HBM if i in any_outputs else pltpu.VMEM)
                for i in range(len(out_shapes))
            ],
            scratch_shapes=list(scratch),
            input_output_aliases=aliases or {},
            compiler_params=pltpu.CompilerParams(vmem_limit_bytes=VMEM_BYTES),
        )(*operands)

    return run


def add_parts(values, parts):
    values = values + parts[0]
    return values + (parts[1] + parts[2]) if len(parts) == 3 else values


def after(value, *earlier):
    return lax.optimization_barrier((value, *earlier))[0]


def shards(forcing, vert_coupling, horiz_coupling, basal_velocity, group_label, ice_mask):
    layers, rows, width_block = vert_coupling.shape
    held, functionals_all, _, width = forcing.shape
    half, functionals = layers // 2, functionals_all // 2
    tiles = lax.axis_size("tile")
    f32 = jnp.float32

    def send(array, target):
        pairs = []
        for t in range(tiles):
            for i in range(4):
                u, k = target(t, i)
                pairs.append((4 * t + i, 4 * u + k))
        return lax.ppermute(array, ("tile", "layer"), pairs)

    def across(array, bits):
        return send(array, lambda t, i: (t, i ^ bits))

    def parity(t):
        return bin(t).count("1") % 2

    def to_near(array, bits=None):
        return to_tile(array, bits, lambda t: t ^ 1)

    def to_far(array, bits=None):
        return to_tile(array, bits, lambda t: t + 1 if t % 2 else t - 1)

    def to_tile(array, bits, partner):
        def target(t, i):
            u = partner(t)
            if not 0 <= u < tiles:
                return t, i ^ 1
            return u, i ^ ((parity(t) + parity(u)) % 2 if bits is None else bits)

        return send(array, target)

    def exchange(values, masks):
        kinds = list(masks)
        if len(masks) == 2:
            kinds.append(masks[0] | masks[1])
        return [send(values, lambda t, i: (t ^ d, i ^ (n < 2))) for n, d in enumerate(kinds)]

    dma = pltpu.SemaphoreType.DMA
    count = layers + 3
    edge_rows = -(-count // 8) * 8
    stack = half * functionals
    flat = (rows, width_block)
    quarter = (held, functionals, rows, width)
    join = lax.optimization_barrier
    block, forcing_sent, forcing_kept = call(
        pack_kernel,
        [(layers + 2, *flat), quarter, quarter],
        [pltpu.VMEM(flat, f32), pltpu.VMEM(flat, jnp.int32), pltpu.VMEM(flat, jnp.int32), dma((6,))],
        hbm_inputs=range(5),
    )(vert_coupling, basal_velocity, group_label, ice_mask, forcing)
    cross, peer, forcing_received = join(
        (across(block, 3), across(block, 1), across(forcing_sent, 1))
    )
    rows_near, rows_far = call(rows_kernel, [(stack, width), (stack, width)])(
        forcing_kept, forcing_received
    )
    rows_far = to_far(rows_far)
    rows_near = to_near(rows_near)
    diag = across(cross, 1)
    planes, edge_near, edge_far = call(
        assemble_kernel, [(count, rows, width), (edge_rows, width), (edge_rows, width)]
    )(block, peer, cross, diag, horiz_coupling)
    edge_far = to_far(edge_far, 1)
    edge_near = to_near(edge_near, 1)

    factors = pltpu.VMEM((2, half, rows, width), f32)
    columns_all = tiles * rows * width
    scale = -((columns_all / GROUPS) ** -0.5)
    (sums_inside,) = call(
        functools.partial(column_kernel, scale=scale),
        [(functionals, GROUPS)],
        [
            pltpu.VMEM((5, layers, rows, width), f32),
            pltpu.VMEM((5, functionals, rows, width), f32),
            pltpu.VMEM((functionals, rows, width), f32),
        ],
    )(forcing_kept, forcing_received, planes)
    planes_later, edge_near, edge_far, sums_inside = join((planes, edge_near, edge_far, sums_inside))
    local, boundary = call(
        local_kernel,
        [(half, functionals, rows, width), (functionals, rows, width)],
        [factors],
    )(forcing_kept, forcing_received, planes)
    sums, halo = call(
        functools.partial(border_kernel, scale=scale),
        [(functionals, GROUPS), (count, 8, width)],
    )(local, planes, edge_near, edge_far, sums_inside)

    boundary_other = across(after(boundary, sums_inside), 3)
    spread, spread_other, response, ends = call(
        coefficient_kernel,
        [(4, half, rows, width), (4, rows, width), (half, rows, width), (6, rows, width)],
        [pltpu.VMEM((2, half, 8, width), f32)],
    )(planes, halo)

    masks = [1 << bit for bit in range(1, (tiles - 1).bit_length())]
    while len(masks) > 2:
        sums = add_parts(sums, exchange(sums, masks[:2]))
        masks = masks[2:]
    parts = exchange(sums, masks)
    base, message = call(
        middle_kernel,
        [(half, functionals, rows, width), (functionals * (rows + 3), width)],
        [factors, pltpu.VMEM((2, half, functionals, width), f32)],
    )(after(local, spread), planes, halo, rows_near, rows_far)
    (message,) = call(fold_kernel, [message.shape])(after(sums, boundary_other), *parts, message)
    message_other = across(message, 3)
    sums = message[functionals * (rows + 2) :]
    near = send(sums, lambda t, i: (t ^ 1, i ^ 1))
    diag = send(sums, lambda t, i: (t ^ 1, i ^ 2))
    message_other, near, diag = join((message_other, near, diag))
    halo_rows_both = pltpu.VMEM((2, functionals, width), f32)
    around, second, sums = call(
        interface_kernel,
        [(4, functionals, rows, width), (functionals, rows, width), (functionals, GROUPS)],
        [halo_rows_both, halo_rows_both],
    )(base, boundary, boundary_other, message, message_other, spread, spread_other, ends, near, diag)
    (sent,) = call(functools.partial(final_kernel, other_core=True), [quarter])(
        base, around, second, spread, response
    )
    (kept,) = call(functools.partial(final_kernel, other_core=False), [quarter])(
        base, around, second, spread, response
    )
    whole = (held, functionals_all, rows, width)
    (partly,) = call(place_kept_kernel, [whole], [dma], any_inputs=(0,), any_outputs=(0,))(kept)
    received, other_sums, partly = join((across(sent, 1), across(sums, 1), partly))
    adjoint, sums = call(
        place_kernel,
        [whole, (functionals_all, GROUPS)],
        [dma((3,))],
        any_inputs=(1, 2, 3),
        hbm_inputs=(0,),
        any_outputs=(0, 1),
        aliases={0: 0},
    )(partly, received, sums, other_sums)
    return (adjoint, sums)


def solution(mesh):
    in_specs = (
        P("layer", None, "tile", None),
        P(None, "tile", "layer"),
        P("tile", None),
        P("tile", "layer"),
        P("tile", "layer"),
        P("tile", "layer"),
    )
    out_specs = (P("layer", None, "tile", None), P())
    return jax.shard_map(shards, mesh=mesh, in_specs=in_specs, out_specs=out_specs, check_vma=False)
```
